256 devices in a mesh: seq: 16 (over y, z_hi, core), tp: 16 (over x, z_lo).
Axes of the slice: x: 4, y: 4, z: 8 (z_hi: 2, z_lo: 4; z = z_hi * 4 + z_lo), core: 2. Of those that a mesh axis runs over, the one named last changes fastest.
Arguments:
- hidden_in: bfloat16 [512, 4608], P(('seq', 'tp')), may hold values from -3 to 3
- query: bfloat16 [512, 4096], P('seq', 'tp'), may hold values from -6 to 6
- kv_pool: bfloat16 [8192, 2, 16, 4, 128], P('seq', None, 'tp'), may hold values from -6 to 6
- kv_map: int32 [512, 16], P(None, 'seq'), may hold values from 0 to 511, as said below
- lengths: int32 [512], replicated, may hold values from 16 to 64
- o_weight: bfloat16 [4096, 4608], P('tp'), may hold values from -0.09375 to 0.09375
- norm_gain: float32 [4608], replicated, may hold values from 0.5 to 1.5
- width_class: int32 [4], replicated, may hold values from 0 to 3, as said below
- gate_weight: bfloat16 [4608, 36864], P(None, ('seq', 'tp')), may hold values from -0.09375 to 0.09375
- up_weight: bfloat16 [4608, 36864], P(None, ('seq', 'tp')), may hold values from -0.09375 to 0.09375
- down_weight: bfloat16 [36864, 4608], P(('seq', 'tp')), may hold values from -0.03125 to 0.03125
Outputs:
- hidden_out: bfloat16 [512, 4608], P(('seq', 'tp'))
The draws below stay inside these ranges and needn't reach their ends.
Inputs may be any that keep to these rules, and one draw needn't show every extreme that they name: Each column of kv_map names every slot from 0 to 511 exactly once. `width_class`: groups g and g + k share a class only when k is a multiple of 4.
All inputs are finite; a program needn't handle non-finite values.
Results may differ from the reference program's by a relative error of at most 0.023.
Values may be sent and summed in bfloat16 or wider, within the bound.
A program may use at most 64 MiB of HBM per device.

```python
import jax
import jax.numpy as jnp
from jax import lax

D = 4608
FF = 36864
QH = 32
KVH = 16
HD = 128
WIDTHS = 4
GROUP = 128
ROWS = 512
CPD = 4
CTX = 64
BLOCKS = 8192
GROUPS = 4
QPRE = 144
N_SEQ = 16


def draw_kv_map(key, part):
    key = jax.random.fold_in(key, 11)
    keys = jax.random.split(key, BLOCKS // ROWS)
    perms = jax.vmap(lambda single: jax.random.permutation(single, ROWS))(keys)
    return jnp.transpose(perms).astype(jnp.int32)


def draw_lengths(key, part):
    key = jax.random.fold_in(key, 23)
    first, second, third = jax.random.split(key, 3)
    base = jax.random.randint(first, (ROWS,), CTX // 4, CTX + 1)
    top_row = jax.random.randint(second, (), 0, ROWS)
    low_row = (top_row + 1 + jax.random.randint(third, (), 0, ROWS - 1)) % ROWS
    return base.at[top_row].set(CTX).at[low_row].set(CTX // 4).astype(jnp.int32)


def draw_width_class(key, part):
    key = jax.random.fold_in(key, 37)
    order = jax.random.permutation(key, WIDTHS).astype(jnp.int32)
    picks = jnp.arange(GROUPS, dtype=jnp.int32) % WIDTHS
    return jnp.take(order, picks).astype(jnp.int32)


def levels(rng, extent, cuts, smallest, largest):
    factor_of, own = 1.0, jax.random.fold_in(rng, 6)
    for dim, blocks in cuts:
        steps = jnp.exp(jax.random.uniform(jax.random.fold_in(own, dim), (blocks,), jnp.float32, smallest / len(cuts), largest / len(cuts)))
        factor_of = factor_of * jnp.repeat(steps, extent[dim] // blocks).reshape([-1 if axis == dim else 1 for axis in range(len(extent))])
    return factor_of


def noise(own_key, dims, spread, reach, shards=(), held_as=jnp.bfloat16):
    values = spread * jax.random.normal(own_key, dims, jnp.float32)
    if shards:
        values = values * levels(own_key, dims, shards, -0.22, 0.18)
    return jnp.clip(values, -reach, reach).astype(held_as)


def setup_inputs(seed: int = 0) -> dict:
    streams_of = jax.random.split(jax.random.key(seed), 12)
    hidden_in = noise(streams_of[0], (ROWS, D), 0.5, 3.0, ((0, 256),))
    query = noise(streams_of[1], (ROWS, QH * HD), 1.0, 6.0, ((0, 16), (1, 16)))
    kv_pool = noise(streams_of[2], (BLOCKS, 2, KVH, CPD, HD), 1.0, 6.0, ((0, 16), (2, 16)))
    kv_map = draw_kv_map(jax.random.fold_in(streams_of[11], 71), 0)
    lengths = draw_lengths(jax.random.fold_in(streams_of[11], 71), 0)
    o_weight = noise(streams_of[5], (QH * HD, D), (QH * HD) ** -0.5, 0.09375, ((0, 16),))
    norm_gain = jnp.clip(jax.random.uniform(streams_of[6], (D,), jnp.float32, 0.5, 1.5), 0.5, 1.5)
    width_class = draw_width_class(jax.random.fold_in(streams_of[11], 71), 0)
    gate_weight = noise(streams_of[8], (D, FF), D ** -0.5, 0.09375, ((1, 256),))
    up_weight = noise(streams_of[9], (D, FF), D ** -0.5, 0.09375, ((1, 256),))
    down_weight = noise(streams_of[10], (FF, D), FF ** -0.5, 0.03125, ((0, 256),))
    return {"hidden_in": hidden_in, "query": query, "kv_pool": kv_pool, "kv_map": kv_map, "lengths": lengths, "o_weight": o_weight, "norm_gain": norm_gain, "width_class": width_class, "gate_weight": gate_weight, "up_weight": up_weight, "down_weight": down_weight}


SOFTCAP = 50.0
EPS = 1e-06

def reference(hidden_in, query, kv_pool, kv_map, lengths, o_weight, norm_gain, width_class, gate_weight, up_weight, down_weight):
    row_ids = jnp.arange(ROWS, dtype=jnp.int32)
    slots = (jnp.arange(N_SEQ, dtype=jnp.int32) * ROWS)[None, :] + kv_map
    positions = jnp.arange(CTX, dtype=jnp.int32)
    live = positions[None, :] < lengths[:, None]
    queries = query.reshape(ROWS, KVH, QH // KVH, HD)

    def one_head(head):
        blocks = kv_pool[:, :, head]
        picked = blocks[slots]
        keys = picked[:, :, 0].reshape(ROWS, CTX, HD).astype(jnp.float32)
        values = picked[:, :, 1].reshape(ROWS, CTX, HD).astype(jnp.float32)
        q_head = lax.dynamic_index_in_dim(queries, head, 1, keepdims=False).astype(jnp.float32)
        scores = jnp.einsum('rgd,rpd->rgp', q_head, keys) * QPRE ** (-0.5)
        capped = SOFTCAP * jnp.tanh(scores / SOFTCAP)
        weights = jnp.where(live[:, None, :], jnp.exp(capped), jnp.float32(0.0))
        totals = lax.optimization_barrier(jnp.sum(weights, axis=2))
        weights_low = lax.optimization_barrier(weights.astype(jnp.bfloat16))
        numer = jnp.einsum('rgp,rpd->rgd', weights_low.astype(jnp.float32), values)
        return (numer, totals)
    numers, totals = lax.map(one_head, jnp.arange(KVH, dtype=jnp.int32))
    attended = numers / totals[..., None]
    attended = jnp.transpose(attended, (1, 0, 2, 3)).reshape(ROWS, QH * HD).astype(jnp.bfloat16)
    projected = jnp.dot(attended, o_weight, preferred_element_type=jnp.float32)
    residual = (hidden_in.astype(jnp.float32) + projected).astype(jnp.bfloat16)
    wide = residual.astype(jnp.float32)
    scale = lax.rsqrt(lax.optimization_barrier(jnp.mean(wide * wide, axis=1, keepdims=True)) + EPS)
    normed = (wide * scale * norm_gain[None, :]).astype(jnp.bfloat16)
    gate = jnp.dot(normed, gate_weight, preferred_element_type=jnp.float32)
    up = jnp.dot(normed, up_weight, preferred_element_type=jnp.float32)
    limit = (width_class[row_ids // GROUP] + 1) * (FF // WIDTHS)
    active = jnp.arange(FF, dtype=jnp.int32)[None, :] < limit[:, None]
    hidden = jnp.where(active, jax.nn.gelu(gate, approximate=True) * up, jnp.float32(0.0)).astype(jnp.bfloat16)
    down = jnp.dot(hidden, down_weight, preferred_element_type=jnp.float32)
    return (residual.astype(jnp.float32) + down).astype(jnp.bfloat16)
```

```python
import functools

import jax
import jax.numpy as jnp
from jax import lax
from jax.experimental import pallas as pl
from jax.experimental.pallas import tpu as pltpu
from jax.sharding import PartitionSpec as P

D = 4608
FF = 36864
WIDTHS = 4
QPRE = 144
SOFTCAP = 50.0
EPS = 1e-06
QD = D // 4
UNITS = FF // 256
MESH = pl.DeviceIdType.MESH
F32 = jnp.float32
BF16 = jnp.bfloat16


def dev(x, y, z, c):
    return (y * 4 + (z // 4) * 2 + c, x * 4 + z % 4)


def dot_nt(a, b):
    return lax.dot_general(a, b, (((1,), (1,)), ((), ())), preferred_element_type=F32)


def remote(src, dst, ssem, rsem, target):
    return pltpu.make_async_remote_copy(
        src_ref=src, dst_ref=dst, send_sem=ssem, recv_sem=rsem, device_id=target, device_id_type=MESH
    )


def kernel(
    hid_ref, q_ref, kvm_ref, len_ref, wc_ref, gain_ref, kv_hbm, ow_hbm, wg_hbm, wu_hbm, wd_hbm,
    out_ref,
    kv_v, ow_v, wg_v, wu_v, wd_v,
    qb, oh, oht, qs, ls, ns, nb, nr, nrx, sb, rb, g, xs, accg, accu, hs, p, r, rx1, t, rx2, zb, rx3, res,
    lsem, a1s, a1r, a3s, a3r, bs, br, c1s, c1r, c2s, c2r, c3s, c3r, cfs, cfr,
    d0s, d0r, d1s, d1r, d2s, d2r, d3s, d3r,
):
    seq = lax.axis_index("seq")
    tp = lax.axis_index("tp")
    y, zh, c = seq // 4, (seq // 2) % 2, seq % 2
    x, zl = tp // 4, tp % 4
    z = zh * 4 + zl
    sib = dev(x, y, z, 1 - c)

    seq_offs = [(dy, dh) for dy in range(4) for dh in range(2) if (dy, dh) != (0, 0)]
    tp_offs = [(dx, dl) for dx in (2, 1, 3, 0) for dl in (2, 1, 3, 0) if (dx, dl) != (0, 0)]
    peers = [sib]
    peers += [dev(x, (y + dy) % 4, ((zh + dh) % 2) * 4 + zl, c) for dy, dh in seq_offs]
    peers += [dev((x + dx) % 4, y, zh * 4 + (zl + dl) % 4, c) for dx, dl in tp_offs]
    peers += [dev(x, y, (1 - zh) * 4 + (zl + dl) % 4, c) for dl in (1, 2, 3)]
    bar = pltpu.get_barrier_semaphore()
    for peer in peers:
        pl.semaphore_signal(bar, inc=1, device_id=peer, device_id_type=MESH)

    loads = [
        pltpu.make_async_copy(kv_hbm, kv_v, lsem.at[0]),
        pltpu.make_async_copy(ow_hbm, ow_v, lsem.at[1]),
        pltpu.make_async_copy(wg_hbm, wg_v, lsem.at[2]),
        pltpu.make_async_copy(wu_hbm, wu_v, lsem.at[3]),
        pltpu.make_async_copy(wd_hbm, wd_v, lsem.at[4]),
    ]
    for load in loads:
        load.start()
    pl.semaphore_wait(bar, len(peers))

    sends = []
    a1 = []
    for i, (dy, dh) in enumerate(seq_offs):
        to = dev(x, (y + dy) % 4, ((zh + dh) % 2) * 4 + zl, c)
        cp = remote(q_ref, qb.at[seq], a1s.at[i], a1r.at[i], to)
        cp.start()
        sends.append(cp)
    cp = remote(q_ref, qb.at[seq], a1s.at[7], a1r.at[7], sib)
    cp.start()
    sends.append(cp)
    qb[seq] = q_ref[...]

    row_id = lax.broadcasted_iota(jnp.int32, (512, 128), 0).astype(F32)
    lane_id = lax.broadcasted_iota(jnp.int32, (128, 128), 1).astype(F32)
    for j in range(4):
        kvrow = kvm_ref[pl.ds(j, 1), :].astype(F32)
        oh[:, pl.ds(j * 128, 128)] = jnp.where(row_id == kvrow, 1.0, 0.0).astype(BF16)
        kvcol = jnp.transpose(jnp.broadcast_to(kvrow, (128, 128)))
        for k in range(4):
            oht[pl.ds(j * 128, 128), pl.ds(k * 128, 128)] = jnp.where(
                kvcol == lane_id + float(k * 128), 1.0, 0.0
            ).astype(BF16)
        lrow = len_ref[pl.ds(j, 1), :].astype(F32)
        xs[pl.ds(j * 128, 128), pl.ds(0, 128)] = jnp.transpose(
            jnp.broadcast_to(lrow, (128, 128))
        ).astype(BF16)
    ls[...] = jnp.dot(oh[...], xs[:, pl.ds(0, 128)], preferred_element_type=F32)

    for i, (dy, dh) in enumerate(seq_offs):
        frm = ((y - dy) % 4) * 4 + ((zh + dh) % 2) * 2 + c
        a = remote(q_ref, qb.at[frm], a1s.at[i], a1r.at[i], sib)
        a.wait_recv()
        cp = remote(qb.at[frm], qb.at[frm], a1s.at[8 + i], a1r.at[8 + i], sib)
        cp.start()
        sends.append(cp)
    remote(q_ref, qb.at[seq], a1s.at[7], a1r.at[7], sib).wait_recv()
    for i, (dy, dh) in enumerate(seq_offs):
        frm = ((y - dy) % 4) * 4 + ((zh + dh) % 2) * 2 + (1 - c)
        remote(qb.at[frm], qb.at[frm], a1s.at[8 + i], a1r.at[8 + i], sib).wait_recv()

    qs[...] = jnp.dot(
        oh[...], qb[...].reshape(512, 256), preferred_element_type=F32
    ).astype(BF16)
    loads[0].wait()

    first = seq * 4
    a_id = lax.broadcasted_iota(jnp.int32, (64, 256), 0) & 31
    b_id = lax.broadcasted_iota(jnp.int32, (64, 256), 1)
    own = (a_id == (b_id >> 3)) & ((b_id & 4) == 0)
    pos = (first + (b_id & 3)).astype(F32)
    lane = lax.broadcasted_iota(jnp.int32, (32, 128), 1)

    def attend(blk, _):
        rows = pl.ds(pl.multiple_of(blk * 32, 32), 32)
        keys = kv_v[pl.ds(pl.multiple_of(blk * 256, 256), 256), :]
        qq = jnp.concatenate([qs[rows, pl.ds(0, 128)], qs[rows, pl.ds(128, 128)]], axis=0)
        s = dot_nt(qq, keys)
        e = jnp.exp(SOFTCAP * jnp.tanh(s * (QPRE ** (-0.5) / SOFTCAP)))
        lb = ls[rows, :]
        lb = jnp.concatenate([lb, lb], axis=0)
        lb = jnp.concatenate([lb, lb], axis=1)
        w = jnp.where(own & (pos < lb), e, 0.0)
        tot = jnp.sum(w, axis=1, keepdims=True)
        wv = pltpu.roll(w, 4, 1).astype(BF16)
        num = jnp.dot(wv, keys, preferred_element_type=F32)
        ns[rows, pl.ds(0, 128)] = num[:32].astype(BF16)
        ns[rows, pl.ds(128, 128)] = num[32:].astype(BF16)
        both = jnp.where((lane & 63) < 32, tot[:32], tot[32:])
        hi = both.astype(BF16).astype(F32)
        ns[rows, pl.ds(256, 128)] = jnp.where(lane < 64, hi, both - hi).astype(BF16)
        return 0

    lax.fori_loop(0, 16, attend, 0)

    for k in range(4):
        v = jnp.dot(
            oht[pl.ds(k * 128, 128), :], ns[...], preferred_element_type=F32
        ).astype(BF16)
        for h in range(2):
            for cc in range(2):
                at = (h * 2 + cc) * 32
                nb[cc, k * 2 + h] = v[at : at + 32]
    cp = remote(nb.at[1 - c], nr, a3s.at[7], a3r.at[7], sib)
    cp.start()
    sends.append(cp)
    cp.wait_recv()

    low_half = lax.broadcasted_iota(jnp.int32, (32, 128), 1) < 64

    def split_total(block):
        both = block + pltpu.roll(block, 64, 1)
        hi = both.astype(BF16).astype(F32)
        return both, jnp.where(low_half, hi, both - hi).astype(BF16)

    def pair_sum(k, _):
        v = nb[c, k].astype(F32) + nr[k].astype(F32)
        nb[c, k, :, pl.ds(0, 256)] = v[:, :256].astype(BF16)
        nb[c, k, :, pl.ds(256, 128)] = split_total(v[:, 256:])[1]
        return 0

    lax.fori_loop(0, 8, pair_sum, 0)
    a3 = []
    for i, (dy, dh) in enumerate(seq_offs):
        yt, ht = (y + dy) % 4, (zh + dh) % 2
        cp = remote(nb.at[c, yt * 2 + ht], nrx.at[i], a3s.at[i], a3r.at[i], dev(x, yt, ht * 4 + zl, c))
        cp.start()
        sends.append(cp)
        a3.append(cp)
    total = nb[c, y * 2 + zh].astype(F32)
    for i in range(7):
        a3[i].wait_recv()
        total = total + nrx[i].astype(F32)
    tot = split_total(total[:, 256:])[0]
    att = jnp.concatenate(
        [total[:, :128] / tot[:, 0:1], total[:, 128:256] / tot[:, 32:33]], axis=1
    ).astype(BF16)

    loads[1].wait()
    rid = lax.broadcasted_iota(jnp.int32, (32, QD), 0)
    row0 = x * 8 + zl * 2
    bcp = []
    for dx in (2, 1, 3, 0):
        xt = (x + dx) % 4
        cols = pl.ds(pl.multiple_of(xt * QD, 128), QD)
        v = jnp.dot(att, ow_v[:, cols], preferred_element_type=F32)
        hid = hid_ref[:, cols].astype(F32)
        v = v + jnp.where(rid == row0, hid[0:1], 0.0) + jnp.where(rid == row0 + 1, hid[1:2], 0.0)
        for b in range(4):
            sb[xt, b] = v[b * 8 : b * 8 + 8].astype(BF16)
        for dl in (2, 1, 3, 0):
            if (dx, dl) == (0, 0):
                continue
            i = tp_offs.index((dx, dl))
            lt = (zl + dl) % 4
            cp = remote(sb.at[xt, lt], rb.at[i], bs.at[i], br.at[i], dev(xt, y, zh * 4 + lt, c))
            cp.start()
            sends.append(cp)
            bcp.append(cp)
    v = sb[x, zl].astype(F32)
    for i in range(15):
        bcp[i].wait_recv()
        v = v + rb[i].astype(F32)
    ia = x * (1 - c) + y * c
    ib = y * (1 - c) + x * c
    g[c, ia, ib, z] = v.astype(BF16)

    for k in range(1, 8):
        own_piece = g.at[c, ia, ib, z]
        cp = remote(own_piece, own_piece, c1s.at[k - 1], c1r.at[k - 1], dev(x, y, (z + k) % 8, c))
        cp.start()
        sends.append(cp)
    for k in range(1, 8):
        piece = g.at[c, ia, ib, (z + 8 - k) % 8]
        remote(piece, piece, c1s.at[k - 1], c1r.at[k - 1], sib).wait_recv()
    for k in (2, 1, 3):
        run = g.at[c, ia, ib]
        cp = remote(
            run, run, c2s.at[k - 1], c2r.at[k - 1], dev((x + k * c) % 4, (y + k * (1 - c)) % 4, z, c)
        )
        cp.start()
        sends.append(cp)
    for k in (1, 3, 2):
        run = g.at[c, ia, (ib + 4 - k) % 4]
        remote(run, run, c2s.at[k - 1], c2r.at[k - 1], sib).wait_recv()
    for k in (2, 1, 3):
        run = g.at[c, ia]
        cp = remote(
            run, run, c3s.at[k - 1], c3r.at[k - 1], dev((x + k * (1 - c)) % 4, (y + k * c) % 4, z, c)
        )
        cp.start()
        sends.append(cp)
    cp = remote(g.at[c, ia], g.at[c, ia], cfs.at[0], cfr.at[0], sib)
    cp.start()
    sends.append(cp)
    for k in (1, 3, 2):
        run = g.at[c, (ia + 4 - k) % 4]
        remote(run, run, c3s.at[k - 1], c3r.at[k - 1], sib).wait_recv()
        cp = remote(run, run, cfs.at[k], cfr.at[k], sib)
        cp.start()
        sends.append(cp)
    ja = x * c + y * (1 - c)
    for k in (0, 1, 3, 2):
        run = g.at[1 - c, (ja + 4 - k) % 4]
        remote(run, run, cfs.at[k], cfr.at[k], sib).wait_recv()

    for load in loads[2:]:
        load.wait()
    row_y = lax.broadcasted_iota(jnp.int32, (256, UNITS), 0) // 64
    row_class = jnp.where(
        row_y == 0, wc_ref[0], jnp.where(row_y == 1, wc_ref[1], jnp.where(row_y == 2, wc_ref[2], wc_ref[3]))
    )
    unit = (seq * 16 + tp) * UNITS + lax.broadcasted_iota(jnp.int32, (256, UNITS), 1)
    active = unit < (row_class + 1) * (FF // WIDTHS)
    for plane in range(2):
        accg[...] = jnp.zeros_like(accg)
        accu[...] = jnp.zeros_like(accu)

        def quarter(k, ss, plane=plane):
            v = g[0, k] if plane == 0 else g[1, :, k]
            f = v.astype(F32).reshape(256, QD)
            at = pl.ds(pl.multiple_of(k * QD, 128), QD)
            u = (f * gain_ref[:, at]).astype(BF16)
            accg[...] += dot_nt(u, wg_v[:, at])
            accu[...] += dot_nt(u, wu_v[:, at])
            return ss + jnp.sum(f * f, axis=1, keepdims=True)

        ss = lax.fori_loop(0, 4, quarter, jnp.zeros((256, 1), F32))
        scale = lax.rsqrt(ss * (1.0 / D) + EPS)
        gate = accg[...] * scale
        up = accu[...] * scale
        act = 0.5 * gate * (1.0 + jnp.tanh(0.7978845608028654 * (gate + 0.044715 * gate * gate * gate)))
        hs[...] = jnp.where(active, act * up, 0.0).astype(BF16)

        def down(k, _, plane=plane):
            at = pl.ds(pl.multiple_of(k * QD, 128), QD)
            v = jnp.dot(hs[...], wd_v[:, at], preferred_element_type=F32)
            v = v.astype(BF16).reshape(4, 2, 4, 8, QD)
            for b in range(4):
                if plane == 0:
                    p[0, b, :, :, :, at] = v[:, :, b]
                else:
                    p[1, :, b, :, :, at] = v[:, :, b]
            return 0

        lax.fori_loop(0, 4, down, 0)

    for k in (2, 1, 3, 0):
        at = (ja + k) % 4
        cp = remote(p.at[1 - c, at], r.at[k], d0s.at[k], d0r.at[k], sib)
        cp.start()
        sends.append(cp)
    for k in (2, 1, 3, 0):
        at = (ia + k) % 4
        remote(p.at[c, at], r.at[k], d0s.at[k], d0r.at[k], sib).wait_recv()

        def add(i, _, at=at, k=k):
            b, h = i // 2, i % 2
            p[c, at, b, h] = (p[c, at, b, h].astype(F32) + r[k, b, h].astype(F32)).astype(BF16)
            return 0

        lax.fori_loop(0, 8, add, 0)
        if k:
            cp = remote(
                p.at[c, at], rx1.at[k - 1], d1s.at[k - 1], d1r.at[k - 1],
                dev((x + k * (1 - c)) % 4, (y + k * c) % 4, z, c),
            )
            cp.start()
            sends.append(cp)

    rid8 = lax.broadcasted_iota(jnp.int32, (8, QD), 0)
    for k in range(4):
        v = g[c, k * (1 - c) + y * c, y * (1 - c) + k * c, zh * 4 + x].astype(F32)
        r0 = jnp.sum(jnp.where(rid8 == zl * 2, v, 0.0), axis=0, keepdims=True)
        r1 = jnp.sum(jnp.where(rid8 == zl * 2 + 1, v, 0.0), axis=0, keepdims=True)
        res[pl.ds(0, 1), pl.ds(k * QD, QD)] = r0
        res[pl.ds(1, 1), pl.ds(k * QD, QD)] = r1

    for k in (1, 3, 2):
        remote(p.at[c, ia], rx1.at[k - 1], d1s.at[k - 1], d1r.at[k - 1], sib).wait_recv()
    for k in (2, 1, 3, 0):
        at = (ib + k) % 4
        for h in range(2):
            v = p[c, ia, at, h].astype(F32)
            for j in range(3):
                v = v + rx1[j, at, h].astype(F32)
            t[at, h] = v.astype(BF16)
        if k:
            cp = remote(
                t.at[at], rx2.at[k - 1], d2s.at[k - 1], d2r.at[k - 1],
                dev((x + k * c) % 4, (y + k * (1 - c)) % 4, z, c),
            )
            cp.start()
            sends.append(cp)
    for k in (1, 3, 2):
        remote(t.at[ib], rx2.at[k - 1], d2s.at[k - 1], d2r.at[k - 1], sib).wait_recv()
    for h in range(2):
        v = t[ib, h].astype(F32)
        for j in range(3):
            v = v + rx2[j, h].astype(F32)
        for b in range(4):
            zb[h * 4 + b] = v[b * 2 : b * 2 + 2].astype(BF16)
    d3 = []
    for k in (4, 3, 5, 2, 6, 1, 7):
        zt = (z + k) % 8
        cp = remote(zb.at[zt], rx3.at[k - 1], d3s.at[k - 1], d3r.at[k - 1], dev(x, y, zt, c))
        cp.start()
        sends.append(cp)
        d3.append(cp)
    v = zb[z].astype(F32)
    for cp in d3:
        cp.wait_recv()
    for k in range(7):
        v = v + rx3[k].astype(F32)
    out_ref[...] = (v + res[...]).astype(BF16)
    for cp in sends:
        cp.wait_send()


def body(
    hidden_in, query, kv_pool, kv_map, lengths, o_weight, norm_gain, width_class,
    gate_weight, up_weight, down_weight,
):
    vmem = pl.BlockSpec(memory_space=pltpu.VMEM)
    hbm = pl.BlockSpec(memory_space=pl.ANY)
    V, S = pltpu.VMEM, pltpu.SemaphoreType.DMA
    scratch = [
        V((4096, 128), BF16), V((256, D), BF16), V((UNITS, D), BF16), V((UNITS, D), BF16), V((UNITS, D), BF16),
        V((16, 32, 256), BF16),
        V((512, 512), BF16),
        V((512, 512), BF16),
        V((512, 256), BF16),
        V((512, 128), F32),
        V((512, 384), BF16),
        V((2, 8, 32, 384), BF16),
        V((8, 32, 384), BF16),
        V((7, 32, 384), BF16),
        V((4, 4, 8, QD), BF16),
        V((15, 8, QD), BF16),
        V((2, 4, 4, 8, 8, QD), BF16),
        V((512, 128), BF16),
        V((256, UNITS), F32), V((256, UNITS), F32),
        V((256, UNITS), BF16),
        V((2, 4, 4, 2, 8, D), BF16),
        V((4, 4, 2, 8, D), BF16),
        V((3, 4, 2, 8, D), BF16),
        V((4, 2, 8, D), BF16),
        V((3, 2, 8, D), BF16),
        V((8, 2, D), BF16),
        V((7, 2, D), BF16),
        V((2, D), F32),
        S((5,)),
        S((15,)), S((15,)), S((8,)), S((8,)), S((15,)), S((15,)),
        S((7,)), S((7,)), S((3,)), S((3,)), S((3,)), S((3,)), S((4,)), S((4,)),
        S((4,)), S((4,)), S((3,)), S((3,)), S((3,)), S((3,)), S((7,)), S((7,)),
    ]
    return pl.pallas_call(
        kernel,
        out_shape=jax.ShapeDtypeStruct((2, D), BF16),
        in_specs=[vmem, vmem, vmem, vmem, pl.BlockSpec(memory_space=pltpu.SMEM), vmem] + [hbm] * 5,
        out_specs=vmem,
        scratch_shapes=scratch,
        compiler_params=pltpu.CompilerParams(
            collective_id=0, has_side_effects=True, vmem_limit_bytes=56 << 20
        ),
        name="layer",
    )(
        hidden_in,
        query,
        kv_map.reshape(4, 128),
        lengths.reshape(4, 128),
        width_class,
        norm_gain.reshape(1, D),
        kv_pool.reshape(4096, 128),
        o_weight,
        jnp.transpose(gate_weight),
        jnp.transpose(up_weight),
        down_weight,
    )


def solution(mesh):
    placed = (
        P(("seq", "tp"), None),
        P("seq", "tp"),
        P("seq", None, "tp", None, None),
        P(None, "seq"),
        P(),
        P("tp", None),
        P(),
        P(),
        P(None, ("seq", "tp")),
        P(None, ("seq", "tp")),
        P(("seq", "tp"), None),
    )
    return jax.shard_map(
        body, mesh=mesh, in_specs=placed, out_specs=P(("seq", "tp"), None), check_vma=False
    )
```

```python
import functools

import jax
import jax.numpy as jnp
from jax import lax
from jax.experimental import pallas as pl
from jax.experimental.pallas import tpu as pltpu
from jax.sharding import PartitionSpec as P

D = 4608
FF = 36864
WIDTHS = 4
QPRE = 144
SOFTCAP = 50.0
EPS = 1e-06
QD = D // 4
UNITS = FF // 256
MESH = pl.DeviceIdType.MESH
F32 = jnp.float32
BF16 = jnp.bfloat16


def dev(x, y, z, c):
    return (y * 4 + (z // 4) * 2 + c, x * 4 + z % 4)


def dot_nt(a, b):
    return lax.dot_general(a, b, (((1,), (1,)), ((), ())), preferred_element_type=F32)


def remote(src, dst, ssem, rsem, target):
    return pltpu.make_async_remote_copy(
        src_ref=src, dst_ref=dst, send_sem=ssem, recv_sem=rsem, device_id=target, device_id_type=MESH
    )


def kernel(
    hid_ref, q_ref, kvm_ref, len_ref, wc_ref, gain_ref, kv_hbm, ow_hbm, wg_hbm, wu_hbm, wd_hbm,
    out_ref,
    kv_v, ow_v, wg_v, wu_v, wd_v,
    qb, oh, oht, qs, ls, ns, nb, nr, nrx, sb, rb, g, xs, accg, accu, ssq, hs, p, r, rx1, t, rx2, zb, rx3, res,
    lsem, a1s, a1r, a3s, a3r, bs, br, c1s, c1r, c2s, c2r, c3s, c3r, cfs, cfr,
    d0s, d0r, d1s, d1r, d2s, d2r, d3s, d3r,
):
    seq = lax.axis_index("seq")
    tp = lax.axis_index("tp")
    y, zh, c = seq // 4, (seq // 2) % 2, seq % 2
    x, zl = tp // 4, tp % 4
    z = zh * 4 + zl
    sib = dev(x, y, z, 1 - c)

    seq_offs = [(dy, dh) for dy in range(4) for dh in range(2) if (dy, dh) != (0, 0)]
    tp_offs = [(dx, dl) for dx in (2, 1, 3, 0) for dl in (2, 1, 3, 0) if (dx, dl) != (0, 0)]
    peers = [sib]
    peers += [dev(x, (y + dy) % 4, ((zh + dh) % 2) * 4 + zl, c) for dy, dh in seq_offs]
    peers += [dev((x + dx) % 4, y, zh * 4 + (zl + dl) % 4, c) for dx, dl in tp_offs]
    peers += [dev(x, y, (1 - zh) * 4 + (zl + dl) % 4, c) for dl in (1, 2, 3)]
    bar = pltpu.get_barrier_semaphore()
    for peer in peers:
        pl.semaphore_signal(bar, inc=1, device_id=peer, device_id_type=MESH)

    loads = [
        pltpu.make_async_copy(kv_hbm, kv_v, lsem.at[0]),
        pltpu.make_async_copy(ow_hbm, ow_v, lsem.at[1]),
        pltpu.make_async_copy(wg_hbm, wg_v, lsem.at[2]),
        pltpu.make_async_copy(wu_hbm, wu_v, lsem.at[3]),
        pltpu.make_async_copy(wd_hbm, wd_v, lsem.at[4]),
    ]
    for load in loads:
        load.start()
    pl.semaphore_wait(bar, len(peers))

    sends = []
    a1 = []
    for i, (dy, dh) in enumerate(seq_offs):
        to = dev(x, (y + dy) % 4, ((zh + dh) % 2) * 4 + zl, c)
        cp = remote(q_ref, qb.at[seq], a1s.at[i], a1r.at[i], to)
        cp.start()
        sends.append(cp)
    cp = remote(q_ref, qb.at[seq], a1s.at[7], a1r.at[7], sib)
    cp.start()
    sends.append(cp)
    qb[seq] = q_ref[...]

    row_id = lax.broadcasted_iota(jnp.int32, (512, 128), 0).astype(F32)
    lane_id = lax.broadcasted_iota(jnp.int32, (128, 128), 1).astype(F32)
    for j in range(4):
        kvrow = kvm_ref[pl.ds(j, 1), :].astype(F32)
        oh[:, pl.ds(j * 128, 128)] = jnp.where(row_id == kvrow, 1.0, 0.0).astype(BF16)
        kvcol = jnp.transpose(jnp.broadcast_to(kvrow, (128, 128)))
        for k in range(4):
            oht[pl.ds(j * 128, 128), pl.ds(k * 128, 128)] = jnp.where(
                kvcol == lane_id + float(k * 128), 1.0, 0.0
            ).astype(BF16)
        lrow = len_ref[pl.ds(j, 1), :].astype(F32)
        xs[pl.ds(j * 128, 128), pl.ds(0, 128)] = jnp.transpose(
            jnp.broadcast_to(lrow, (128, 128))
        ).astype(BF16)
    ls[...] = jnp.dot(oh[...], xs[:, pl.ds(0, 128)], preferred_element_type=F32)

    for i, (dy, dh) in enumerate(seq_offs):
        frm = ((y - dy) % 4) * 4 + ((zh + dh) % 2) * 2 + c
        a = remote(q_ref, qb.at[frm], a1s.at[i], a1r.at[i], sib)
        a.wait_recv()
        cp = remote(qb.at[frm], qb.at[frm], a1s.at[8 + i], a1r.at[8 + i], sib)
        cp.start()
        sends.append(cp)
    remote(q_ref, qb.at[seq], a1s.at[7], a1r.at[7], sib).wait_recv()
    for i, (dy, dh) in enumerate(seq_offs):
        frm = ((y - dy) % 4) * 4 + ((zh + dh) % 2) * 2 + (1 - c)
        remote(qb.at[frm], qb.at[frm], a1s.at[8 + i], a1r.at[8 + i], sib).wait_recv()

    qs[...] = jnp.dot(
        oh[...], qb[...].reshape(512, 256), preferred_element_type=F32
    ).astype(BF16)
    loads[0].wait()

    first = seq * 4
    a_id = lax.broadcasted_iota(jnp.int32, (64, 256), 0) & 31
    b_id = lax.broadcasted_iota(jnp.int32, (64, 256), 1)
    own = (a_id == (b_id >> 3)) & ((b_id & 4) == 0)
    pos = (first + (b_id & 3)).astype(F32)
    lane = lax.broadcasted_iota(jnp.int32, (32, 128), 1)

    def attend(blk, _):
        rows = pl.ds(pl.multiple_of(blk * 32, 32), 32)
        keys = kv_v[pl.ds(pl.multiple_of(blk * 256, 256), 256), :]
        qq = jnp.concatenate([qs[rows, pl.ds(0, 128)], qs[rows, pl.ds(128, 128)]], axis=0)
        s = dot_nt(qq, keys)
        e = jnp.exp(SOFTCAP * jnp.tanh(s * (QPRE ** (-0.5) / SOFTCAP)))
        lb = ls[rows, :]
        lb = jnp.concatenate([lb, lb], axis=0)
        lb = jnp.concatenate([lb, lb], axis=1)
        w = jnp.where(own & (pos < lb), e, 0.0)
        tot = jnp.sum(w, axis=1, keepdims=True)
        wv = pltpu.roll(w, 4, 1).astype(BF16)
        num = jnp.dot(wv, keys, preferred_element_type=F32)
        ns[rows, pl.ds(0, 128)] = num[:32].astype(BF16)
        ns[rows, pl.ds(128, 128)] = num[32:].astype(BF16)
        both = jnp.where((lane & 63) < 32, tot[:32], tot[32:])
        hi = both.astype(BF16).astype(F32)
        ns[rows, pl.ds(256, 128)] = jnp.where(lane < 64, hi, both - hi).astype(BF16)
        return 0

    lax.fori_loop(0, 16, attend, 0, unroll=4)

    for k in range(4):
        v = jnp.dot(
            oht[pl.ds(k * 128, 128), :], ns[...], preferred_element_type=F32
        ).astype(BF16)
        for h in range(2):
            for cc in range(2):
                at = (h * 2 + cc) * 32
                nb[cc, k * 2 + h] = v[at : at + 32]
    cp = remote(nb.at[1 - c], nr, a3s.at[7], a3r.at[7], sib)
    cp.start()
    sends.append(cp)
    cp.wait_recv()

    low_half = lax.broadcasted_iota(jnp.int32, (32, 128), 1) < 64

    def split_total(block):
        both = block + pltpu.roll(block, 64, 1)
        hi = both.astype(BF16).astype(F32)
        return both, jnp.where(low_half, hi, both - hi).astype(BF16)

    def pair_sum(k, _):
        v = nb[c, k].astype(F32) + nr[k].astype(F32)
        nb[c, k, :, pl.ds(0, 256)] = v[:, :256].astype(BF16)
        nb[c, k, :, pl.ds(256, 128)] = split_total(v[:, 256:])[1]
        return 0

    lax.fori_loop(0, 8, pair_sum, 0)
    a3 = []
    for i, (dy, dh) in enumerate(seq_offs):
        yt, ht = (y + dy) % 4, (zh + dh) % 2
        cp = remote(nb.at[c, yt * 2 + ht], nrx.at[i], a3s.at[i], a3r.at[i], dev(x, yt, ht * 4 + zl, c))
        cp.start()
        sends.append(cp)
        a3.append(cp)
    total = nb[c, y * 2 + zh].astype(F32)
    for i in range(7):
        a3[i].wait_recv()
        total = total + nrx[i].astype(F32)
    tot = split_total(total[:, 256:])[0]
    att = jnp.concatenate(
        [total[:, :128] / tot[:, 0:1], total[:, 128:256] / tot[:, 32:33]], axis=1
    ).astype(BF16)

    loads[1].wait()
    rid = lax.broadcasted_iota(jnp.int32, (32, QD), 0)
    row0 = x * 8 + zl * 2
    bcp = []
    for dx in (2, 1, 3, 0):
        xt = (x + dx) % 4
        cols = pl.ds(pl.multiple_of(xt * QD, 128), QD)
        v = jnp.dot(att, ow_v[:, cols], preferred_element_type=F32)
        hid = hid_ref[:, cols].astype(F32)
        v = v + jnp.where(rid == row0, hid[0:1], 0.0) + jnp.where(rid == row0 + 1, hid[1:2], 0.0)
        for b in range(4):
            sb[xt, b] = v[b * 8 : b * 8 + 8].astype(BF16)
        for dl in (2, 1, 3, 0):
            if (dx, dl) == (0, 0):
                continue
            i = tp_offs.index((dx, dl))
            lt = (zl + dl) % 4
            cp = remote(sb.at[xt, lt], rb.at[i], bs.at[i], br.at[i], dev(xt, y, zh * 4 + lt, c))
            cp.start()
            sends.append(cp)
            bcp.append(cp)
    v = sb[x, zl].astype(F32)
    for i in range(15):
        bcp[i].wait_recv()
        v = v + rb[i].astype(F32)
    outer, inner = (x, y), (y, x)
    own_piece = g.at[c, zh, x * (1 - zh) + y * zh, y * (1 - zh) + x * zh, zl]
    own_piece[...] = v.astype(BF16)

    def step(h, along_outer, k):
        if (h == 0) == along_outer:
            return dev((x + k) % 4, y, z, c)
        return dev(x, (y + k) % 4, z, c)

    def push(src, dst, ssem, rsem, to):
        cp = remote(src, dst, ssem, rsem, to)
        cp.start()
        sends.append(cp)

    for k in (4, 3, 5, 2, 6, 1, 7):
        push(own_piece, own_piece, c1s.at[k - 1], c1r.at[k - 1], dev(x, y, (z + k) % 8, c))
    accg[...] = jnp.zeros_like(accg)
    accu[...] = jnp.zeros_like(accu)
    ssq[...] = jnp.zeros_like(ssq)
    for load in loads[2:]:
        load.wait()
    for k in (1, 7, 2, 6, 3, 5, 4):
        frm = (z + 8 - k) % 8
        fh = frm // 4
        piece = g.at[c, fh, x * (1 - fh) + y * fh, y * (1 - fh) + x * fh, frm % 4]
        remote(piece, piece, c1s.at[k - 1], c1r.at[k - 1], sib).wait_recv()
    for k in (1, 3, 2):
        for h in range(2):
            run = g.at[c, h, outer[h], inner[h]]
            push(run, run, c2s.at[h, k - 1], c2r.at[h, k - 1], step(h, False, k))
    for k in (1, 3, 2):
        for h in range(2):
            run = g.at[c, h, outer[h], inner[h]]
            push(run, run, c3s.at[h, 0, k - 1], c3r.at[h, 0, k - 1], step(h, True, k))
    for j in (1, 3, 2):
        for h in range(2):
            run = g.at[c, h, outer[h], (inner[h] + 4 - j) % 4]
            remote(run, run, c2s.at[h, j - 1], c2r.at[h, j - 1], sib).wait_recv()
            for k in (1, 3):
                push(run, run, c3s.at[h, j, k - 1], c3r.at[h, j, k - 1], step(h, True, k))
    for j in (1, 3, 2):
        for h in range(2):
            run = g.at[c, h, outer[h], (inner[h] + 4 - j) % 4]
            push(run, run, c3s.at[h, j, 1], c3r.at[h, j, 1], step(h, True, 2))
    for h in range(2):
        run = g.at[c, h, outer[h]]
        push(run, run, cfs.at[h, 0], cfr.at[h, 0], sib)

    def partial(h, f, xq, at):
        cols = pl.ds(pl.multiple_of(xq * QD, 128), QD)
        u = (f * gain_ref[:, cols]).astype(BF16)
        accg[h, at, :] += dot_nt(u, wg_v[:, cols])
        accu[h, at, :] += dot_nt(u, wu_v[:, cols])
        ssq[h, at, :] += jnp.sum(f * f, axis=1, keepdims=True)

    def first_half(plane, xq):
        f = g[plane, 0, xq].astype(F32).reshape(128, QD)
        partial(0, f, xq, pl.ds(pl.multiple_of(plane * 128, 128), 128))

    def from_sibling(h, k):
        run = g.at[1 - c, h, (outer[h] + 4 - k) % 4]
        remote(run, run, cfs.at[h, k], cfr.at[h, k], sib).wait_recv()

    first_half(c, x)
    for h in range(2):
        from_sibling(h, 0)
    first_half(1 - c, x)
    for k in (1, 3, 2):
        for h in range(2):
            for j in (0, 1, 3, 2):
                run = g.at[c, h, (outer[h] + 4 - k) % 4, (inner[h] + 4 - j) % 4]
                remote(run, run, c3s.at[h, j, k - 1], c3r.at[h, j, k - 1], sib).wait_recv()
            run = g.at[c, h, (outer[h] + 4 - k) % 4]
            push(run, run, cfs.at[h, k], cfr.at[h, k], sib)
        first_half(c, (x + 4 - k) % 4)
        if k == 2:
            from_sibling(1, k)
        for h in range(2):
            if (h, k) != (1, 2):
                from_sibling(h, k)
        first_half(1 - c, (x + 4 - k) % 4)

    def second_half(xq, _):
        f = g[:, 1, :, xq].astype(F32).reshape(256, QD)
        partial(1, f, xq, pl.ds(0, 256))
        return 0

    lax.fori_loop(0, 4, second_half, 0)

    row_y = (lax.broadcasted_iota(jnp.int32, (128, UNITS), 0) >> 5) & 3
    row_class = jnp.where(
        row_y == 0, wc_ref[0], jnp.where(row_y == 1, wc_ref[1], jnp.where(row_y == 2, wc_ref[2], wc_ref[3]))
    )
    unit = (seq * 16 + tp) * UNITS + lax.broadcasted_iota(jnp.int32, (128, UNITS), 1)
    active = unit < (row_class + 1) * (FF // WIDTHS)

    def activate(i, _):
        h, plane = i // 2, i % 2
        at = pl.ds(pl.multiple_of(plane * 128, 128), 128)
        scale = lax.rsqrt(ssq[h, at, :] * (1.0 / D) + EPS)
        gate = accg[h, at, :] * scale
        up = accu[h, at, :] * scale
        act = 0.5 * gate * (1.0 + jnp.tanh(0.7978845608028654 * (gate + 0.044715 * gate * gate * gate)))
        hs[plane, pl.ds(pl.multiple_of(h * 128, 128), 128), :] = jnp.where(active, act * up, 0.0).astype(BF16)
        return 0

    lax.fori_loop(0, 4, activate, 0)

    def down(plane, k):
        cols = pl.ds(pl.multiple_of(k * QD, 128), QD)
        v = jnp.dot(hs[plane], wd_v[:, cols], preferred_element_type=F32)
        v = v.astype(BF16).reshape(2, 4, 4, 8, QD)
        for w in range(4):
            p[plane, k, 0, w] = v[0, :, w]
        p[plane, k, 1] = v[1]

    def d0(k):
        return remote(p.at[1 - c, k], r.at[k], d0s.at[k], d0r.at[k], sib)

    def d1(k, h, off):
        return remote(
            p.at[c, k, h, (outer[h] + off) % 4], rx1.at[k, h, off - 1],
            d1s.at[k, h, off - 1], d1r.at[k, h, off - 1], step(h, True, off),
        )

    def d2(k, h, off):
        return remote(
            t.at[k, h, (inner[h] + off) % 4], rx2.at[k, h, off - 1],
            d2s.at[k, h, off - 1], d2r.at[k, h, off - 1], step(h, False, off),
        )

    def pair(k):
        d0(k).wait_recv()

        def add(i, _):
            h, a = i // 4, i % 4
            p[c, k, h, a] = (p[c, k, h, a].astype(F32) + r[k, h, a].astype(F32)).astype(BF16)
            return 0

        lax.fori_loop(0, 8, add, 0)
        for off in (2, 1, 3):
            for h in range(2):
                d1(k, h, off).start()

    def produce(k, _):
        down(1 - c, k)
        d0(k).start()
        down(c, k)

        @pl.when(k > 0)
        def _():
            pair(k - 1)

        return 0

    lax.fori_loop(0, 4, produce, 0)
    pair(3)

    rid8 = lax.broadcasted_iota(jnp.int32, (8, QD), 0)

    def own_rows(k, _):
        v = g[c, zh, k * (1 - zh) + y * zh, y * (1 - zh) + k * zh, x].astype(F32)
        cols = pl.ds(pl.multiple_of(k * QD, 128), QD)
        res[pl.ds(0, 1), cols] = jnp.sum(jnp.where(rid8 == zl * 2, v, 0.0), axis=0, keepdims=True)
        res[pl.ds(1, 1), cols] = jnp.sum(jnp.where(rid8 == zl * 2 + 1, v, 0.0), axis=0, keepdims=True)
        return 0

    lax.fori_loop(0, 4, own_rows, 0)

    def outer_sum(k, _):
        for h in range(2):
            for off in (1, 3, 2):
                d1(k, h, off).wait_recv()
            v = p[c, k, h, outer[h]].astype(F32)
            for j in range(3):
                v = v + rx1[k, h, j].astype(F32)
            t[k, h] = v.astype(BF16)
            for off in (2, 1, 3):
                d2(k, h, off).start()
        return 0

    lax.fori_loop(0, 4, outer_sum, 0)

    def inner_sum(k, _):
        cols = pl.ds(pl.multiple_of(k * QD, 128), QD)
        for h in range(2):
            for off in (1, 3, 2):
                d2(k, h, off).wait_recv()
            v = t[k, h, inner[h]].astype(F32)
            for j in range(3):
                v = v + rx2[k, h, j].astype(F32)
            for b in range(4):
                zb[h * 4 + b, :, cols] = v[b * 2 : b * 2 + 2].astype(BF16)
        return 0

    lax.fori_loop(0, 4, inner_sum, 0)
    d3 = []
    for k in (4, 3, 5, 2, 6, 1, 7):
        zt = (z + k) % 8
        cp = remote(zb.at[zt], rx3.at[k - 1], d3s.at[k - 1], d3r.at[k - 1], dev(x, y, zt, c))
        cp.start()
        sends.append(cp)
        d3.append(cp)
    v = zb[z].astype(F32) + res[...]
    for cp in d3:
        cp.wait_recv()
    for k in range(7):
        v = v + rx3[k].astype(F32)
    out_ref[...] = v.astype(BF16)
    for cp in sends:
        cp.wait_send()

    def drain(k, _):
        d0(k).wait_send()
        for h in range(2):
            for off in (1, 2, 3):
                d1(k, h, off).wait_send()
                d2(k, h, off).wait_send()
        return 0

    lax.fori_loop(0, 4, drain, 0)


def body(
    hidden_in, query, kv_pool, kv_map, lengths, o_weight, norm_gain, width_class,
    gate_weight, up_weight, down_weight,
):
    vmem = pl.BlockSpec(memory_space=pltpu.VMEM)
    hbm = pl.BlockSpec(memory_space=pl.ANY)
    V, S = pltpu.VMEM, pltpu.SemaphoreType.DMA
    scratch = [
        V((4096, 128), BF16), V((256, D), BF16), V((UNITS, D), BF16), V((UNITS, D), BF16), V((UNITS, D), BF16),
        V((16, 32, 256), BF16),
        V((512, 512), BF16),
        V((512, 512), BF16),
        V((512, 256), BF16),
        V((512, 128), F32),
        V((512, 384), BF16),
        V((2, 8, 32, 384), BF16),
        V((8, 32, 384), BF16),
        V((7, 32, 384), BF16),
        V((4, 4, 8, QD), BF16),
        V((15, 8, QD), BF16),
        V((2, 2, 4, 4, 4, 8, QD), BF16),
        V((512, 128), BF16),
        V((2, 256, UNITS), F32), V((2, 256, UNITS), F32),
        V((2, 256, 1), F32),
        V((2, 256, UNITS), BF16),
        V((2, 4, 2, 4, 4, 8, QD), BF16),
        V((4, 2, 4, 4, 8, QD), BF16),
        V((4, 2, 3, 4, 8, QD), BF16),
        V((4, 2, 4, 8, QD), BF16),
        V((4, 2, 3, 8, QD), BF16),
        V((8, 2, D), BF16),
        V((7, 2, D), BF16),
        V((2, D), F32),
        S((5,)),
        S((15,)), S((15,)), S((8,)), S((8,)), S((15,)), S((15,)),
        S((7,)), S((7,)), S((2, 3)), S((2, 3)), S((2, 4, 3)), S((2, 4, 3)), S((2, 4)), S((2, 4)),
        S((4,)), S((4,)), S((4, 2, 3)), S((4, 2, 3)), S((4, 2, 3)), S((4, 2, 3)), S((7,)), S((7,)),
    ]
    return pl.pallas_call(
        kernel,
        out_shape=jax.ShapeDtypeStruct((2, D), BF16),
        in_specs=[vmem, vmem, vmem, vmem, pl.BlockSpec(memory_space=pltpu.SMEM), vmem] + [hbm] * 5,
        out_specs=vmem,
        scratch_shapes=scratch,
        compiler_params=pltpu.CompilerParams(
            collective_id=0, has_side_effects=True, vmem_limit_bytes=56 << 20
        ),
        name="layer",
    )(
        hidden_in,
        query,
        kv_map.reshape(4, 128),
        lengths.reshape(4, 128),
        width_class,
        norm_gain.reshape(1, D),
        kv_pool.reshape(4096, 128),
        o_weight,
        jnp.transpose(gate_weight),
        jnp.transpose(up_weight),
        down_weight,
    )


def solution(mesh):
    placed = (
        P(("seq", "tp"), None),
        P("seq", "tp"),
        P("seq", None, "tp", None, None),
        P(None, "seq"),
        P(),
        P("tp", None),
        P(),
        P(),
        P(None, ("seq", "tp")),
        P(None, ("seq", "tp")),
        P(("seq", "tp"), None),
    )
    return jax.shard_map(
        body, mesh=mesh, in_specs=placed, out_specs=P(("seq", "tp"), None), check_vma=False
    )
```

```python
import functools

import jax
import jax.numpy as jnp
from jax import lax
from jax.experimental import pallas as pl
from jax.experimental.pallas import tpu as pltpu
from jax.sharding import PartitionSpec as P

D = 4608
FF = 36864
WIDTHS = 4
QPRE = 144
SOFTCAP = 50.0
EPS = 1e-06
QD = D // 4
UNITS = FF // 256
MESH = pl.DeviceIdType.MESH
F32 = jnp.float32
BF16 = jnp.bfloat16


def dev(x, y, z, c):
    return (y * 4 + (z // 4) * 2 + c, x * 4 + z % 4)


def dot_nt(a, b):
    return lax.dot_general(a, b, (((1,), (1,)), ((), ())), preferred_element_type=F32)


def remote(src, dst, ssem, rsem, target):
    return pltpu.make_async_remote_copy(
        src_ref=src, dst_ref=dst, send_sem=ssem, recv_sem=rsem, device_id=target, device_id_type=MESH
    )


def kernel(
    hid_ref, q_ref, kvm_ref, len_ref, wc_ref, gain_ref, kv_hbm, ow_hbm, wg_hbm, wu_hbm, wd_hbm,
    out_ref,
    kv_v, ow_v, wgu_v, wd_v,
    qb, oh, oht, qs, ls, ns, nb, nr, nrx, sb, rb, g, xs, acc, ssq, hs, p, rx1, t, rx2, zb, rx3, res, gain, kvt, vs,
    lsem, a1s, a1r, a3s, a3r, bs, br, c1s, c1r, c2s, c2r, c3s, c3r,
    wxs, wxr, d1s, d1r, d2s, d2r, d3s, d3r,
):
    seq = lax.axis_index("seq")
    tp = lax.axis_index("tp")
    y, zh, c = seq // 4, (seq // 2) % 2, seq % 2
    x, zl = tp // 4, tp % 4
    z = zh * 4 + zl
    sib = dev(x, y, z, 1 - c)

    seq_offs = [(dy, dh) for dy in range(4) for dh in range(2) if (dy, dh) != (0, 0)]
    tp_offs = [(dx, dl) for dx in (2, 1, 3, 0) for dl in (2, 1, 3, 0) if (dx, dl) != (0, 0)]
    peers = [sib]
    peers += [dev(x, (y + dy) % 4, ((zh + dh) % 2) * 4 + zl, c) for dy, dh in seq_offs]
    peers += [dev((x + dx) % 4, y, zh * 4 + (zl + dl) % 4, c) for dx, dl in tp_offs]
    peers += [dev(x, y, (1 - zh) * 4 + (zl + dl) % 4, c) for dl in (1, 2, 3)]
    bar = pltpu.get_barrier_semaphore()
    for peer in peers:
        pl.semaphore_signal(bar, inc=1, device_id=peer, device_id_type=MESH)

    loads = [
        pltpu.make_async_copy(kv_hbm, kv_v, lsem.at[0]),
        pltpu.make_async_copy(ow_hbm, ow_v, lsem.at[1]),
        pltpu.make_async_copy(wg_hbm, wgu_v.at[0, c], lsem.at[2]),
        pltpu.make_async_copy(wu_hbm, wgu_v.at[1, c], lsem.at[3]),
        pltpu.make_async_copy(wd_hbm, wd_v.at[c], lsem.at[4]),
    ]
    for load in loads:
        load.start()
    pl.semaphore_wait(bar, len(peers))

    sends = []
    a1 = []
    for i, (dy, dh) in enumerate(seq_offs):
        to = dev(x, (y + dy) % 4, ((zh + dh) % 2) * 4 + zl, c)
        cp = remote(q_ref, qb.at[seq], a1s.at[i], a1r.at[i], to)
        cp.start()
        sends.append(cp)
    cp = remote(q_ref, qb.at[seq], a1s.at[7], a1r.at[7], sib)
    cp.start()
    sends.append(cp)
    qb[seq] = q_ref[...]

    row_id = lax.broadcasted_iota(jnp.int32, (512, 128), 0).astype(F32)
    lane_id = lax.broadcasted_iota(jnp.int32, (128, 128), 1).astype(F32)
    for j in range(4):
        kvrow = kvm_ref[pl.ds(j, 1), :].astype(F32)
        oh[:, pl.ds(j * 128, 128)] = jnp.where(row_id == kvrow, 1.0, 0.0).astype(BF16)
        kvcol = jnp.transpose(jnp.broadcast_to(kvrow, (128, 128)))
        for k in range(4):
            oht[pl.ds(j * 128, 128), pl.ds(k * 128, 128)] = jnp.where(
                kvcol == lane_id + float(k * 128), 1.0, 0.0
            ).astype(BF16)
        lrow = len_ref[pl.ds(j, 1), :].astype(F32)
        xs[pl.ds(j * 128, 128), pl.ds(0, 128)] = jnp.transpose(
            jnp.broadcast_to(lrow, (128, 128))
        ).astype(BF16)
    for j in range(36):
        gain[:, pl.ds(j * 128, 128)] = gain_ref[pl.ds(j, 1), :]
    ls[...] = jnp.dot(oh[...], xs[:, pl.ds(0, 128)], preferred_element_type=F32)

    loads[0].wait()

    def prepare(blk, _):
        rows = pl.ds(pl.multiple_of(blk * 256, 256), 256)
        block = kv_v[rows, :].astype(F32)
        kvt[:, rows] = jnp.transpose(block).astype(BF16)
        vs[rows, pl.ds(0, 128)] = pltpu.roll(block, 252, 0).astype(BF16)
        vs[rows, pl.ds(128, 128)] = jnp.ones((256, 128), BF16)
        return 0

    lax.fori_loop(0, 16, prepare, 0)
    for i, (dy, dh) in enumerate(seq_offs):
        frm = ((y - dy) % 4) * 4 + ((zh + dh) % 2) * 2 + c
        a = remote(q_ref, qb.at[frm], a1s.at[i], a1r.at[i], sib)
        a.wait_recv()
        cp = remote(qb.at[frm], qb.at[frm], a1s.at[8 + i], a1r.at[8 + i], sib)
        cp.start()
        sends.append(cp)
    remote(q_ref, qb.at[seq], a1s.at[7], a1r.at[7], sib).wait_recv()
    for i, (dy, dh) in enumerate(seq_offs):
        frm = ((y - dy) % 4) * 4 + ((zh + dh) % 2) * 2 + (1 - c)
        remote(qb.at[frm], qb.at[frm], a1s.at[8 + i], a1r.at[8 + i], sib).wait_recv()

    weights = [
        remote(wg_hbm, wgu_v.at[0, c], wxs.at[0], wxr.at[0], sib),
        remote(wu_hbm, wgu_v.at[1, c], wxs.at[1], wxr.at[1], sib),
        remote(wd_hbm, wd_v.at[c], wxs.at[2], wxr.at[2], sib),
    ]
    sends += weights
    weights[0].start()
    qs[...] = jnp.dot(
        oh[...], qb[...].reshape(512, 256), preferred_element_type=F32
    ).astype(BF16)

    first = seq * 4
    a_id = lax.broadcasted_iota(jnp.int32, (64, 256), 0) & 31
    b_id = lax.broadcasted_iota(jnp.int32, (64, 256), 1)
    own = (a_id == (b_id >> 3)) & ((b_id & 4) == 0)
    pos = (first + (b_id & 3)).astype(F32)
    lane = lax.broadcasted_iota(jnp.int32, (32, 128), 1)

    def attend(blk, _):
        rows = pl.ds(pl.multiple_of(blk * 32, 32), 32)
        span = pl.ds(pl.multiple_of(blk * 256, 256), 256)
        qq = jnp.concatenate([qs[rows, pl.ds(0, 128)], qs[rows, pl.ds(128, 128)]], axis=0)
        s = jnp.dot(qq, kvt[:, span], preferred_element_type=F32)
        e = jnp.exp(SOFTCAP * jnp.tanh(s * (QPRE ** (-0.5) / SOFTCAP)))
        lb = ls[rows, :]
        lb = jnp.concatenate([lb, lb], axis=0)
        lb = jnp.concatenate([lb, lb], axis=1)
        w = jnp.where(own & (pos < lb), e, 0.0)
        low = w.astype(BF16)
        rest = (w - low.astype(F32)).astype(BF16)
        num = jnp.dot(jnp.concatenate([low, rest], axis=0), vs[span, :], preferred_element_type=F32)
        ns[rows, pl.ds(0, 128)] = num[:32, :128].astype(BF16)
        ns[rows, pl.ds(128, 128)] = num[32:64, :128].astype(BF16)
        tot = num[:64, 128:] + num[64:, 128:]
        both = jnp.where((lane & 63) < 32, tot[:32], tot[32:])
        hi = both.astype(BF16).astype(F32)
        ns[rows, pl.ds(256, 128)] = jnp.where(lane < 64, hi, both - hi).astype(BF16)
        return 0

    lax.fori_loop(0, 16, attend, 0, unroll=4)

    for k in range(4):
        v = jnp.dot(
            oht[pl.ds(k * 128, 128), :], ns[...], preferred_element_type=F32
        ).astype(BF16)
        for h in range(2):
            for cc in range(2):
                at = (h * 2 + cc) * 32
                nb[cc, k * 2 + h] = v[at : at + 32]
    cp = remote(nb.at[1 - c], nr, a3s.at[7], a3r.at[7], sib)
    cp.start()
    sends.append(cp)
    cp.wait_recv()

    low_half = lax.broadcasted_iota(jnp.int32, (32, 128), 1) < 64

    def split_total(block):
        both = block + pltpu.roll(block, 64, 1)
        hi = both.astype(BF16).astype(F32)
        return both, jnp.where(low_half, hi, both - hi).astype(BF16)

    def pair_sum(k, _):
        v = nb[c, k].astype(F32) + nr[k].astype(F32)
        nb[c, k, :, pl.ds(0, 256)] = v[:, :256].astype(BF16)
        nb[c, k, :, pl.ds(256, 128)] = split_total(v[:, 256:])[1]
        return 0

    lax.fori_loop(0, 8, pair_sum, 0)
    a3 = []
    for i, (dy, dh) in enumerate(seq_offs):
        yt, ht = (y + dy) % 4, (zh + dh) % 2
        cp = remote(nb.at[c, yt * 2 + ht], nrx.at[i], a3s.at[i], a3r.at[i], dev(x, yt, ht * 4 + zl, c))
        cp.start()
        sends.append(cp)
        a3.append(cp)
    weights[1].start()
    total = nb[c, y * 2 + zh].astype(F32)
    for i in range(7):
        a3[i].wait_recv()
        total = total + nrx[i].astype(F32)
    tot = split_total(total[:, 256:])[0]
    att = jnp.concatenate(
        [total[:, :128] / tot[:, 0:1], total[:, 128:256] / tot[:, 32:33]], axis=1
    ).astype(BF16)

    loads[1].wait()
    rid = lax.broadcasted_iota(jnp.int32, (32, QD), 0)
    row0 = x * 8 + zl * 2
    bcp = []
    for dx in (2, 1, 3, 0):
        xt = (x + dx) % 4
        cols = pl.ds(pl.multiple_of(xt * QD, 128), QD)
        v = jnp.dot(att, ow_v[:, cols], preferred_element_type=F32)
        hid = hid_ref[:, cols].astype(F32)
        v = v + jnp.where(rid == row0, hid[0:1], 0.0) + jnp.where(rid == row0 + 1, hid[1:2], 0.0)
        for b in range(4):
            sb[xt, b] = v[b * 8 : b * 8 + 8].astype(BF16)
        for dl in (2, 1, 3, 0):
            if (dx, dl) == (0, 0):
                continue
            i = tp_offs.index((dx, dl))
            lt = (zl + dl) % 4
            cp = remote(sb.at[xt, lt], rb.at[i], bs.at[i], br.at[i], dev(xt, y, zh * 4 + lt, c))
            cp.start()
            sends.append(cp)
            bcp.append(cp)
    weights[2].start()
    v = sb[x, zl].astype(F32)
    for i in range(15):
        bcp[i].wait_recv()
        v = v + rb[i].astype(F32)
    outer, inner = (x, y), (y, x)
    own_piece = g.at[zh, x * (1 - zh) + y * zh, y * (1 - zh) + x * zh, zl]
    own_piece[...] = v.astype(BF16)

    def step(h, along_outer, k):
        if (h == 0) == along_outer:
            return dev((x + k) % 4, y, z, c)
        return dev(x, (y + k) % 4, z, c)

    def push(src, dst, ssem, rsem, to):
        cp = remote(src, dst, ssem, rsem, to)
        cp.start()
        sends.append(cp)

    for k in (4, 3, 5, 2, 6, 1, 7):
        push(own_piece, own_piece, c1s.at[k - 1], c1r.at[k - 1], dev(x, y, (z + k) % 8, c))
    acc[...] = jnp.zeros_like(acc)
    ssq[...] = jnp.zeros_like(ssq)
    for load in loads[2:]:
        load.wait()
    for weight in weights:
        weight.wait_recv()
    for k in (1, 7, 2, 6, 3, 5, 4):
        frm = (z + 8 - k) % 8
        fh = frm // 4
        piece = g.at[fh, x * (1 - fh) + y * fh, y * (1 - fh) + x * fh, frm % 4]
        remote(piece, piece, c1s.at[k - 1], c1r.at[k - 1], sib).wait_recv()
    for k in (1, 3, 2):
        for h in range(2):
            run = g.at[h, outer[h], inner[h]]
            push(run, run, c2s.at[h, k - 1], c2r.at[h, k - 1], step(h, False, k))
    for k in (1, 3, 2):
        for h in range(2):
            run = g.at[h, outer[h], inner[h]]
            push(run, run, c3s.at[h, 0, k - 1], c3r.at[h, 0, k - 1], step(h, True, k))
    for j in (1, 3, 2):
        for h in range(2):
            run = g.at[h, outer[h], (inner[h] + 4 - j) % 4]
            remote(run, run, c2s.at[h, j - 1], c2r.at[h, j - 1], sib).wait_recv()
            for k in (1, 3):
                push(run, run, c3s.at[h, j, k - 1], c3r.at[h, j, k - 1], step(h, True, k))
    for j in (1, 3, 2):
        for h in range(2):
            run = g.at[h, outer[h], (inner[h] + 4 - j) % 4]
            push(run, run, c3s.at[h, j, 1], c3r.at[h, j, 1], step(h, True, 2))

    def partial(h, f, xq):
        cols = pl.ds(pl.multiple_of(xq * QD, 128), QD)
        u = (f.astype(F32).reshape(128, QD) * gain[:, cols]).astype(BF16)
        acc[h] += dot_nt(u, wgu_v[:, :, :, cols].reshape(4 * UNITS, QD))

    def squares(h, f):
        f = f.astype(F32).reshape(128, QD)
        ssq[h] += jnp.sum(f * f, axis=1, keepdims=True)

    def first_half(xq):
        partial(0, g[0, xq], xq)
        squares(0, g[0, xq])

    first_half(x)
    for k in (1, 3, 2):
        for h in range(2):
            for j in (0, 1, 3, 2):
                run = g.at[h, (outer[h] + 4 - k) % 4, (inner[h] + 4 - j) % 4]
                remote(run, run, c3s.at[h, j, k - 1], c3r.at[h, j, k - 1], sib).wait_recv()
        first_half((x + 4 - k) % 4)

    def second_half(xq, _):
        partial(1, g[1, :, xq], xq)
        squares(1, g[1, :, xq])
        return 0

    lax.fori_loop(0, 4, second_half, 0)

    row_y = lax.broadcasted_iota(jnp.int32, (128, 2 * UNITS), 0) >> 5
    row_class = jnp.where(
        row_y == 0, wc_ref[0], jnp.where(row_y == 1, wc_ref[1], jnp.where(row_y == 2, wc_ref[2], wc_ref[3]))
    )
    unit_id = lax.broadcasted_iota(jnp.int32, (128, 2 * UNITS), 1)
    pair_base = ((seq - c) * 16 + tp) * UNITS
    unit = pair_base + unit_id + jnp.where(unit_id >= UNITS, 15 * UNITS, 0)
    active = unit < (row_class + 1) * (FF // WIDTHS)
    for h in range(2):
        scale = lax.rsqrt(ssq[h] * (1.0 / D) + EPS)
        gate = acc[h, :, : 2 * UNITS] * scale
        up = acc[h, :, 2 * UNITS :] * scale
        act = 0.5 * gate * (1.0 + jnp.tanh(0.7978845608028654 * (gate + 0.044715 * gate * gate * gate)))
        hs[pl.ds(h * 128, 128), :] = jnp.where(active, act * up, 0.0).astype(BF16)

    def d1(k, h, off):
        return remote(
            p.at[k, h, (outer[h] + off) % 4], rx1.at[k, h, off - 1],
            d1s.at[k, h, off - 1], d1r.at[k, h, off - 1], step(h, True, off),
        )

    def d2(k, h, off):
        return remote(
            t.at[k, h, (inner[h] + off) % 4], rx2.at[k, h, off - 1],
            d2s.at[k, h, off - 1], d2r.at[k, h, off - 1], step(h, False, off),
        )

    def produce(k, _):
        cols = pl.ds(pl.multiple_of(k * QD, 128), QD)
        v = jnp.dot(hs[...], wd_v[:, :, cols].reshape(2 * UNITS, QD), preferred_element_type=F32)
        v = v.astype(BF16).reshape(2, 4, 4, 8, QD)
        for w in range(4):
            p[k, 0, w] = v[0, :, w]
        p[k, 1] = v[1]
        for off in (2, 1, 3):
            for h in range(2):
                d1(k, h, off).start()
        return 0

    lax.fori_loop(0, 4, produce, 0)

    rid8 = lax.broadcasted_iota(jnp.int32, (8, QD), 0)

    def own_rows(k, _):
        v = g[zh, k * (1 - zh) + y * zh, y * (1 - zh) + k * zh, x].astype(F32)
        cols = pl.ds(pl.multiple_of(k * QD, 128), QD)
        res[pl.ds(0, 1), cols] = jnp.sum(jnp.where(rid8 == zl * 2, v, 0.0), axis=0, keepdims=True)
        res[pl.ds(1, 1), cols] = jnp.sum(jnp.where(rid8 == zl * 2 + 1, v, 0.0), axis=0, keepdims=True)
        return 0

    lax.fori_loop(0, 4, own_rows, 0)

    def outer_sum(k, _):
        for h in range(2):
            for off in (1, 3, 2):
                d1(k, h, off).wait_recv()
            v = p[k, h, outer[h]].astype(F32)
            for j in range(3):
                v = v + rx1[k, h, j].astype(F32)
            t[k, h] = v.astype(BF16)
            for off in (2, 1, 3):
                d2(k, h, off).start()
        return 0

    lax.fori_loop(0, 4, outer_sum, 0)

    def inner_sum(k, _):
        cols = pl.ds(pl.multiple_of(k * QD, 128), QD)
        for h in range(2):
            for off in (1, 3, 2):
                d2(k, h, off).wait_recv()
            v = t[k, h, inner[h]].astype(F32)
            for j in range(3):
                v = v + rx2[k, h, j].astype(F32)
            for b in range(4):
                zb[h * 4 + b, :, cols] = v[b * 2 : b * 2 + 2].astype(BF16)
        return 0

    lax.fori_loop(0, 4, inner_sum, 0)
    d3 = []
    for k in (4, 3, 5, 2, 6, 1, 7):
        zt = (z + k) % 8
        cp = remote(zb.at[zt], rx3.at[k - 1], d3s.at[k - 1], d3r.at[k - 1], dev(x, y, zt, c))
        cp.start()
        sends.append(cp)
        d3.append(cp)
    v = zb[z].astype(F32) + res[...]
    for cp in d3:
        cp.wait_recv()
    for k in range(7):
        v = v + rx3[k].astype(F32)
    out_ref[...] = v.astype(BF16)
    for cp in sends:
        cp.wait_send()

    def drain(k, _):
        for h in range(2):
            for off in (1, 2, 3):
                d1(k, h, off).wait_send()
                d2(k, h, off).wait_send()
        return 0

    lax.fori_loop(0, 4, drain, 0)


def body(
    hidden_in, query, kv_pool, kv_map, lengths, o_weight, norm_gain, width_class,
    gate_weight, up_weight, down_weight,
):
    vmem = pl.BlockSpec(memory_space=pltpu.VMEM)
    hbm = pl.BlockSpec(memory_space=pl.ANY)
    V, S = pltpu.VMEM, pltpu.SemaphoreType.DMA
    scratch = [
        V((4096, 128), BF16), V((256, D), BF16), V((2, 2, UNITS, D), BF16), V((2, UNITS, D), BF16),
        V((16, 32, 256), BF16),
        V((512, 512), BF16),
        V((512, 512), BF16),
        V((512, 256), BF16),
        V((512, 128), F32),
        V((512, 384), BF16),
        V((2, 8, 32, 384), BF16),
        V((8, 32, 384), BF16),
        V((7, 32, 384), BF16),
        V((4, 4, 8, QD), BF16),
        V((15, 8, QD), BF16),
        V((2, 4, 4, 4, 8, QD), BF16),
        V((512, 128), BF16),
        V((2, 128, 4 * UNITS), F32),
        V((2, 128, 1), F32),
        V((256, 2 * UNITS), BF16),
        V((4, 2, 4, 4, 8, QD), BF16),
        V((4, 2, 3, 4, 8, QD), BF16),
        V((4, 2, 4, 8, QD), BF16),
        V((4, 2, 3, 8, QD), BF16),
        V((8, 2, D), BF16),
        V((7, 2, D), BF16),
        V((2, D), F32),
        V((1, D), F32),
        V((128, 4096), BF16),
        V((4096, 256), BF16),
        S((5,)),
        S((15,)), S((15,)), S((8,)), S((8,)), S((15,)), S((15,)),
        S((7,)), S((7,)), S((2, 3)), S((2, 3)), S((2, 4, 3)), S((2, 4, 3)),
        S((3,)), S((3,)), S((4, 2, 3)), S((4, 2, 3)), S((4, 2, 3)), S((4, 2, 3)), S((7,)), S((7,)),
    ]
    return pl.pallas_call(
        kernel,
        out_shape=jax.ShapeDtypeStruct((2, D), BF16),
        in_specs=[vmem, vmem, vmem, vmem, pl.BlockSpec(memory_space=pltpu.SMEM), vmem] + [hbm] * 5,
        out_specs=vmem,
        scratch_shapes=scratch,
        compiler_params=pltpu.CompilerParams(
            collective_id=0, has_side_effects=True, vmem_limit_bytes=56 << 20
        ),
        name="layer",
    )(
        hidden_in,
        query,
        kv_map.reshape(4, 128),
        lengths.reshape(4, 128),
        width_class,
        norm_gain.reshape(36, 128),
        kv_pool.reshape(4096, 128),
        o_weight,
        jnp.transpose(gate_weight),
        jnp.transpose(up_weight),
        down_weight,
    )


def solution(mesh):
    placed = (
        P(("seq", "tp"), None),
        P("seq", "tp"),
        P("seq", None, "tp", None, None),
        P(None, "seq"),
        P(),
        P("tp", None),
        P(),
        P(),
        P(None, ("seq", "tp")),
        P(None, ("seq", "tp")),
        P(("seq", "tp"), None),
    )
    return jax.shard_map(
        body, mesh=mesh, in_specs=placed, out_specs=P(("seq", "tp"), None), check_vma=False
    )
```

```python
import functools

import jax
import jax.numpy as jnp
from jax import lax
from jax.experimental import pallas as pl
from jax.experimental.pallas import tpu as pltpu
from jax.sharding import PartitionSpec as P

D = 4608
FF = 36864
WIDTHS = 4
QPRE = 144
SOFTCAP = 50.0
EPS = 1e-06
QD = D // 4
UNITS = FF // 256
MESH = pl.DeviceIdType.MESH
F32 = jnp.float32
BF16 = jnp.bfloat16


def dev(x, y, z, c):
    return (y * 4 + (z // 4) * 2 + c, x * 4 + z % 4)


def dot_nt(a, b):
    return lax.dot_general(a, b, (((1,), (1,)), ((), ())), preferred_element_type=F32)


def remote(src, dst, ssem, rsem, target):
    return pltpu.make_async_remote_copy(
        src_ref=src, dst_ref=dst, send_sem=ssem, recv_sem=rsem, device_id=target, device_id_type=MESH
    )


def kernel(
    hid_hbm, q_hbm, kvm_hbm, len_hbm, wc_hbm, gain_hbm, kv_hbm, ow_hbm, wg_hbm, wu_hbm, wd_hbm,
    out_ref,
    hid_ref, kvm_ref, len_ref, wc_ref, gain_ref, kv_v, ow_v, wgu_v, wd_v,
    qb, oh, oht, qs, ls, ns, nb, nr, nrx, sb, rb, g, xs, acc, ssq, hs, p, rl, rx1, t, rx2, zb, rx3, res, gain, kvt, vs,
    lsem, a1s, a1r, a3s, a3r, bs, br, c1s, c1r, c2s, c2r, c3s, c3r,
    wxs, wxr, d0s, d0r, d1s, d1r, d2s, d2r, d3s, d3r,
):
    seq = lax.axis_index("seq")
    tp = lax.axis_index("tp")
    y, zh, c = seq // 4, (seq // 2) % 2, seq % 2
    x, zl = tp // 4, tp % 4
    z = zh * 4 + zl
    sib = dev(x, y, z, 1 - c)

    seq_offs = [(2, 1), (1, 1), (3, 1), (0, 1), (2, 0), (1, 0), (3, 0)]
    tp_offs = [(dx, dl) for dx in (2, 1, 3, 0) for dl in (2, 1, 3, 0) if (dx, dl) != (0, 0)]
    peers = [sib]
    peers += [dev(x, (y + dy) % 4, ((zh + dh) % 2) * 4 + zl, c) for dy, dh in seq_offs]
    peers += [dev((x + dx) % 4, y, zh * 4 + (zl + dl) % 4, c) for dx, dl in tp_offs]
    peers += [dev(x, y, (1 - zh) * 4 + (zl + dl) % 4, c) for dl in (1, 2, 3)]
    bar = pltpu.get_barrier_semaphore()
    for peer in peers:
        pl.semaphore_signal(bar, inc=1, device_id=peer, device_id_type=MESH)

    loads = [
        pltpu.make_async_copy(kv_hbm, kv_v, lsem.at[0]),
        pltpu.make_async_copy(ow_hbm, ow_v, lsem.at[1]),
        pltpu.make_async_copy(wg_hbm, wgu_v.at[0, c], lsem.at[2]),
        pltpu.make_async_copy(wu_hbm, wgu_v.at[1, c], lsem.at[3]),
        pltpu.make_async_copy(wd_hbm, wd_v.at[c], lsem.at[4]),
    ]
    small = [
        pltpu.make_async_copy(q_hbm, qb.at[seq], lsem.at[5]),
        pltpu.make_async_copy(kvm_hbm, kvm_ref, lsem.at[6]),
        pltpu.make_async_copy(len_hbm, len_ref, lsem.at[7]),
        pltpu.make_async_copy(gain_hbm, gain_ref, lsem.at[8]),
        pltpu.make_async_copy(hid_hbm, hid_ref, lsem.at[9]),
        pltpu.make_async_copy(wc_hbm, wc_ref, lsem.at[10]),
    ]
    for load in small + loads:
        load.start()
    for load in small:
        load.wait()
    pl.semaphore_wait(bar, len(peers))

    sends = []
    a1 = []
    for i, (dy, dh) in enumerate(seq_offs):
        to = dev(x, (y + dy) % 4, ((zh + dh) % 2) * 4 + zl, c)
        cp = remote(qb.at[seq], qb.at[seq], a1s.at[i], a1r.at[i], to)
        cp.start()
        sends.append(cp)
    cp = remote(qb.at[seq], qb.at[seq], a1s.at[7], a1r.at[7], sib)
    cp.start()
    sends.append(cp)

    row_id = lax.broadcasted_iota(jnp.int32, (512, 128), 0).astype(F32)
    lane_id = lax.broadcasted_iota(jnp.int32, (128, 128), 1).astype(F32)
    for j in range(4):
        kvrow = kvm_ref[pl.ds(j, 1), :].astype(F32)
        oh[:, pl.ds(j * 128, 128)] = jnp.where(row_id == kvrow, 1.0, 0.0).astype(BF16)
        kvcol = jnp.transpose(jnp.broadcast_to(kvrow, (128, 128)))
        for k in range(4):
            oht[pl.ds(j * 128, 128), pl.ds(k * 128, 128)] = jnp.where(
                kvcol == lane_id + float(k * 128), 1.0, 0.0
            ).astype(BF16)
        lrow = len_ref[pl.ds(j, 1), :].astype(F32)
        xs[pl.ds(j * 128, 128), pl.ds(0, 128)] = jnp.transpose(
            jnp.broadcast_to(lrow, (128, 128))
        ).astype(BF16)
    for j in range(36):
        gain[:, pl.ds(j * 128, 128)] = gain_ref[pl.ds(j, 1), :]
    ls[...] = jnp.dot(oh[...], xs[:, pl.ds(0, 128)], preferred_element_type=F32)

    loads[0].wait()

    def prepare(blk, _):
        rows = pl.ds(pl.multiple_of(blk * 256, 256), 256)
        block = kv_v[rows, :].astype(F32)
        kvt[:, rows] = jnp.transpose(block).astype(BF16)
        vs[rows, pl.ds(0, 128)] = pltpu.roll(block, 252, 0).astype(BF16)
        vs[rows, pl.ds(128, 128)] = jnp.ones((256, 128), BF16)
        return 0

    lax.fori_loop(0, 16, prepare, 0)
    for i, (dy, dh) in reversed(list(enumerate(seq_offs))):
        frm = ((y - dy) % 4) * 4 + ((zh + dh) % 2) * 2 + c
        a = remote(qb.at[seq], qb.at[frm], a1s.at[i], a1r.at[i], sib)
        a.wait_recv()
        cp = remote(qb.at[frm], qb.at[frm], a1s.at[8 + i], a1r.at[8 + i], sib)
        cp.start()
        sends.append(cp)
    remote(qb.at[seq], qb.at[seq], a1s.at[7], a1r.at[7], sib).wait_recv()
    for i, (dy, dh) in enumerate(seq_offs):
        frm = ((y - dy) % 4) * 4 + ((zh + dh) % 2) * 2 + (1 - c)
        remote(qb.at[frm], qb.at[frm], a1s.at[8 + i], a1r.at[8 + i], sib).wait_recv()

    weights = [
        remote(wg_hbm, wgu_v.at[0, c], wxs.at[0], wxr.at[0], sib),
        remote(wu_hbm, wgu_v.at[1, c], wxs.at[1], wxr.at[1], sib),
        remote(wd_hbm, wd_v.at[c], wxs.at[2], wxr.at[2], sib),
    ]
    sends += weights
    weights[0].start()
    qs[...] = jnp.dot(
        oh[...], qb[...].reshape(512, 256), preferred_element_type=F32
    ).astype(BF16)

    first = seq * 4
    a_id = lax.broadcasted_iota(jnp.int32, (64, 256), 0) & 31
    b_id = lax.broadcasted_iota(jnp.int32, (64, 256), 1)
    own = (a_id == (b_id >> 3)) & ((b_id & 4) == 0)
    pos = (first + (b_id & 3)).astype(F32)
    lane = lax.broadcasted_iota(jnp.int32, (32, 128), 1)

    def attend(blk, _):
        rows = pl.ds(pl.multiple_of(blk * 32, 32), 32)
        span = pl.ds(pl.multiple_of(blk * 256, 256), 256)
        qq = jnp.concatenate([qs[rows, pl.ds(0, 128)], qs[rows, pl.ds(128, 128)]], axis=0)
        s = jnp.dot(qq, kvt[:, span], preferred_element_type=F32)
        e = jnp.exp(SOFTCAP * jnp.tanh(s * (QPRE ** (-0.5) / SOFTCAP)))
        lb = ls[rows, :]
        lb = jnp.concatenate([lb, lb], axis=0)
        lb = jnp.concatenate([lb, lb], axis=1)
        w = jnp.where(own & (pos < lb), e, 0.0)
        low = w.astype(BF16)
        rest = (w - low.astype(F32)).astype(BF16)
        num = jnp.dot(jnp.concatenate([low, rest], axis=0), vs[span, :], preferred_element_type=F32)
        ns[rows, pl.ds(0, 128)] = num[:32, :128].astype(BF16)
        ns[rows, pl.ds(128, 128)] = num[32:64, :128].astype(BF16)
        tot = num[:64, 128:] + num[64:, 128:]
        both = jnp.where((lane & 63) < 32, tot[:32], tot[32:])
        hi = both.astype(BF16).astype(F32)
        ns[rows, pl.ds(256, 128)] = jnp.where(lane < 64, hi, both - hi).astype(BF16)
        return 0

    lax.fori_loop(0, 16, attend, 0, unroll=4)

    for k in range(4):
        v = jnp.dot(
            oht[pl.ds(k * 128, 128), :], ns[...], preferred_element_type=F32
        ).astype(BF16)
        for h in range(2):
            for cc in range(2):
                at = (h * 2 + cc) * 32
                nb[cc, k * 2 + h] = v[at : at + 32]
    cp = remote(nb.at[1 - c], nr, a3s.at[7], a3r.at[7], sib)
    cp.start()
    sends.append(cp)
    cp.wait_recv()

    low_half = lax.broadcasted_iota(jnp.int32, (32, 128), 1) < 64

    def split_total(block):
        both = block + pltpu.roll(block, 64, 1)
        hi = both.astype(BF16).astype(F32)
        return both, jnp.where(low_half, hi, both - hi).astype(BF16)

    def pair_sum(k):
        v = nb[c, k].astype(F32) + nr[k].astype(F32)
        nb[c, k, :, pl.ds(0, 256)] = v[:, :256].astype(BF16)
        nb[c, k, :, pl.ds(256, 128)] = split_total(v[:, 256:])[1]

    a3 = []
    for i, (dy, dh) in enumerate(seq_offs):
        yt, ht = (y + dy) % 4, (zh + dh) % 2
        pair_sum(yt * 2 + ht)
        cp = remote(nb.at[c, yt * 2 + ht], nrx.at[i], a3s.at[i], a3r.at[i], dev(x, yt, ht * 4 + zl, c))
        cp.start()
        sends.append(cp)
        a3.append(cp)
    pair_sum(y * 2 + zh)
    weights[1].start()
    total = nb[c, y * 2 + zh].astype(F32)
    for i in reversed(range(7)):
        a3[i].wait_recv()
        total = total + nrx[i].astype(F32)
    tot = split_total(total[:, 256:])[0]
    att = jnp.concatenate(
        [total[:, :128] / tot[:, 0:1], total[:, 128:256] / tot[:, 32:33]], axis=1
    ).astype(BF16)

    loads[1].wait()
    rid = lax.broadcasted_iota(jnp.int32, (32, QD), 0)
    row0 = x * 8 + zl * 2
    bcp = []
    for dx in (2, 1, 3, 0):
        xt = (x + dx) % 4
        cols = pl.ds(pl.multiple_of(xt * QD, 128), QD)
        v = jnp.dot(att, ow_v[:, cols], preferred_element_type=F32)
        hid = hid_ref[:, cols].astype(F32)
        v = v + jnp.where(rid == row0, hid[0:1], 0.0) + jnp.where(rid == row0 + 1, hid[1:2], 0.0)
        for b in range(4):
            sb[xt, b] = v[b * 8 : b * 8 + 8].astype(BF16)
        for dl in (2, 1, 3, 0):
            if (dx, dl) == (0, 0):
                continue
            i = tp_offs.index((dx, dl))
            lt = (zl + dl) % 4
            cp = remote(sb.at[xt, lt], rb.at[i], bs.at[i], br.at[i], dev(xt, y, zh * 4 + lt, c))
            cp.start()
            sends.append(cp)
            bcp.append(cp)
    weights[2].start()
    v = sb[x, zl].astype(F32)
    for i in range(15):
        bcp[i].wait_recv()
        v = v + rb[i].astype(F32)
    outer, inner = (x, y), (y, x)
    own_piece = g.at[zh, x * (1 - zh) + y * zh, y * (1 - zh) + x * zh, zl]
    own_piece[...] = v.astype(BF16)

    def step(h, along_outer, k):
        if (h == 0) == along_outer:
            return dev((x + k) % 4, y, z, c)
        return dev(x, (y + k) % 4, z, c)

    def push(src, dst, ssem, rsem, to):
        cp = remote(src, dst, ssem, rsem, to)
        cp.start()
        sends.append(cp)

    for k in (4, 3, 5, 2, 6, 1, 7):
        push(own_piece, own_piece, c1s.at[k - 1], c1r.at[k - 1], dev(x, y, (z + k) % 8, c))
    acc[...] = jnp.zeros_like(acc)
    ssq[...] = jnp.zeros_like(ssq)
    for load in loads[2:]:
        load.wait()
    for weight in weights:
        weight.wait_recv()
    for half, blocks in ((zh, [(zl + d) % 4 for d in (1, 3, 2)]), (1 - zh, range(4))):
        ho, hi_ = x * (1 - half) + y * half, y * (1 - half) + x * half
        for m in blocks:
            k = (z + 7 - half * 4 - m) % 8
            piece = g.at[half, ho, hi_, m]
            remote(piece, piece, c1s.at[k], c1r.at[k], sib).wait_recv()
        run = g.at[half, ho, hi_]
        for k in (1, 3, 2):
            to = dev((x + k * half) % 4, (y + k * (1 - half)) % 4, z, c)
            push(run, run, c2s.at[half, k - 1], c2r.at[half, k - 1], to)
        for k in (1, 3):
            to = dev((x + k * (1 - half)) % 4, (y + k * half) % 4, z, c)
            push(run, run, c3s.at[half, 0, k - 1], c3r.at[half, 0, k - 1], to)

    def arrived(h, j, k):
        run = g.at[h, (outer[h] + 4 - k) % 4, (inner[h] + 4 - j) % 4]
        remote(run, run, c3s.at[h, j, k - 1], c3r.at[h, j, k - 1], sib).wait_recv()
        return run

    def relay(j, k):
        for h in range(2):
            run = arrived(h, j, k)
            push(run, run, c3s.at[h, j, 1], c3r.at[h, j, 1], step(h, True, k))

    for j in (1, 3, 2):
        for h in range(2):
            run = g.at[h, outer[h], (inner[h] + 4 - j) % 4]
            remote(run, run, c2s.at[h, j - 1], c2r.at[h, j - 1], sib).wait_recv()
            for k in (1, 3):
                push(run, run, c3s.at[h, j, k - 1], c3r.at[h, j, k - 1], step(h, True, k))
    relay(0, 1)

    def partial(h, f, xq):
        cols = pl.ds(pl.multiple_of(xq * QD, 128), QD)
        u = (f.astype(F32).reshape(128, QD) * gain[:, cols]).astype(BF16)
        acc[h] += dot_nt(u, wgu_v[:, :, :, cols].reshape(4 * UNITS, QD))

    def squares(h, f):
        f = f.astype(F32).reshape(128, QD)
        ssq[h] += jnp.sum(f * f, axis=1, keepdims=True)

    def first_half(xq):
        partial(0, g[0, xq], xq)
        squares(0, g[0, xq])

    first_half(x)
    relay(3, 3)
    relay(1, 1)
    relay(2, 3)
    rest = {1: (3, 2), 3: (0, 1), 2: (0, 3, 1, 2)}
    for k in (1, 3, 2):
        for j in rest[k]:
            arrived(0, j, k)
        first_half((x + 4 - k) % 4)
    for k in (1, 3, 2):
        for j in rest[k]:
            arrived(1, j, k)

    def second_half(xq, _):
        partial(1, g[1, :, xq], xq)
        squares(1, g[1, :, xq])
        return 0

    lax.fori_loop(0, 4, second_half, 0)

    row_y = lax.broadcasted_iota(jnp.int32, (128, 2 * UNITS), 0) >> 5
    row_class = jnp.where(
        row_y == 0, wc_ref[0], jnp.where(row_y == 1, wc_ref[1], jnp.where(row_y == 2, wc_ref[2], wc_ref[3]))
    )
    unit_id = lax.broadcasted_iota(jnp.int32, (128, 2 * UNITS), 1)
    pair_base = ((seq - c) * 16 + tp) * UNITS
    unit = pair_base + unit_id + jnp.where(unit_id >= UNITS, 15 * UNITS, 0)
    active = unit < (row_class + 1) * (FF // WIDTHS)
    for h in range(2):
        scale = lax.rsqrt(ssq[h] * (1.0 / D) + EPS)
        gate = acc[h, :, : 2 * UNITS] * scale
        up = acc[h, :, 2 * UNITS :] * scale
        act = 0.5 * gate * (1.0 + jnp.tanh(0.7978845608028654 * (gate + 0.044715 * gate * gate * gate)))
        hs[pl.ds(h * 128, 128), :] = jnp.where(active, act * up, 0.0).astype(BF16)

    def along(k):
        return jnp.where(k < 2, 0, 1)

    def d0(k, h):
        return remote(
            p.at[k, h, (outer[h] + 2) % 4], rl.at[k, h], d0s.at[k, h], d0r.at[k, h],
            step(h, True, 1 + 2 * along(k)),
        )

    def d1(k, h, way):
        off = 1 + 2 * way
        return remote(
            p.at[k, h, (outer[h] + off) % 4], rx1.at[k, h, way],
            d1s.at[k, h, way], d1r.at[k, h, way], step(h, True, off),
        )

    def d2(k, h, off):
        return remote(
            t.at[k, h, (inner[h] + off) % 4], rx2.at[k, h, off - 1],
            d2s.at[k, h, off - 1], d2r.at[k, h, off - 1], step(h, False, off),
        )

    def produce(i, _):
        k = (i % 2) * 2 + i // 2
        cols = pl.ds(pl.multiple_of(k * QD, 128), QD)
        v = jnp.dot(hs[...], wd_v[:, :, cols].reshape(2 * UNITS, QD), preferred_element_type=F32)
        v = v.astype(BF16).reshape(2, 4, 4, 8, QD)
        for w in range(4):
            p[k, 0, w] = v[0, :, w]
        p[k, 1] = v[1]
        for h in range(2):
            d0(k, h).start()
            d1(k, h, 1 - along(k)).start()
        return 0

    lax.fori_loop(0, 4, produce, 0)

    def combine(i, _):
        k = (i % 2) * 2 + i // 2
        for h in range(2):
            d0(k, h).wait_recv()
            at = (outer[h] + 1 + 2 * along(k)) % 4
            p[k, h, at] = (p[k, h, at].astype(F32) + rl[k, h].astype(F32)).astype(BF16)
            d1(k, h, along(k)).start()
        return 0

    lax.fori_loop(0, 4, combine, 0)

    rid8 = lax.broadcasted_iota(jnp.int32, (8, QD), 0)

    def own_rows(k, _):
        v = g[zh, k * (1 - zh) + y * zh, y * (1 - zh) + k * zh, x].astype(F32)
        cols = pl.ds(pl.multiple_of(k * QD, 128), QD)
        res[pl.ds(0, 1), cols] = jnp.sum(jnp.where(rid8 == zl * 2, v, 0.0), axis=0, keepdims=True)
        res[pl.ds(1, 1), cols] = jnp.sum(jnp.where(rid8 == zl * 2 + 1, v, 0.0), axis=0, keepdims=True)
        return 0

    lax.fori_loop(0, 4, own_rows, 0)

    def outer_sum(i, _):
        k = (i % 2) * 2 + i // 2
        for h in range(2):
            for way in range(2):
                d1(k, h, way).wait_recv()
            v = p[k, h, outer[h]].astype(F32)
            for j in range(2):
                v = v + rx1[k, h, j].astype(F32)
            t[k, h] = v.astype(BF16)
            for off in (2, 1, 3):
                d2(k, h, off).start()
        return 0

    lax.fori_loop(0, 4, outer_sum, 0)

    def inner_sum(k, _):
        cols = pl.ds(pl.multiple_of(k * QD, 128), QD)
        for h in range(2):
            for off in (1, 3, 2):
                d2(k, h, off).wait_recv()
            v = t[k, h, inner[h]].astype(F32)
            for j in range(3):
                v = v + rx2[k, h, j].astype(F32)
            for b in range(4):
                zb[h * 4 + b, :, cols] = v[b * 2 : b * 2 + 2].astype(BF16)
        return 0

    lax.fori_loop(0, 4, inner_sum, 0)
    d3 = []
    for k in (4, 3, 5, 2, 6, 1, 7):
        zt = (z + k) % 8
        cp = remote(zb.at[zt], rx3.at[k - 1], d3s.at[k - 1], d3r.at[k - 1], dev(x, y, zt, c))
        cp.start()
        sends.append(cp)
        d3.append(cp)
    v = zb[z].astype(F32) + res[...]
    for cp in d3:
        cp.wait_recv()
    for k in range(7):
        v = v + rx3[k].astype(F32)
    out_ref[...] = v.astype(BF16)
    for cp in sends:
        cp.wait_send()

    def drain(k, _):
        for h in range(2):
            d0(k, h).wait_send()
            for way in range(2):
                d1(k, h, way).wait_send()
            for off in (1, 2, 3):
                d2(k, h, off).wait_send()
        return 0

    lax.fori_loop(0, 4, drain, 0)


def body(
    hidden_in, query, kv_pool, kv_map, lengths, o_weight, norm_gain, width_class,
    gate_weight, up_weight, down_weight,
):
    vmem = pl.BlockSpec(memory_space=pltpu.VMEM)
    hbm = pl.BlockSpec(memory_space=pl.ANY)
    V, S = pltpu.VMEM, pltpu.SemaphoreType.DMA
    scratch = [
        V((2, D), BF16), V((4, 128), jnp.int32), V((4, 128), jnp.int32), pltpu.SMEM((4,), jnp.int32),
        V((36, 128), F32),
        V((4096, 128), BF16), V((256, D), BF16), V((2, 2, UNITS, D), BF16), V((2, UNITS, D), BF16),
        V((16, 32, 256), BF16),
        V((512, 512), BF16),
        V((512, 512), BF16),
        V((512, 256), BF16),
        V((512, 128), F32),
        V((512, 384), BF16),
        V((2, 8, 32, 384), BF16),
        V((8, 32, 384), BF16),
        V((7, 32, 384), BF16),
        V((4, 4, 8, QD), BF16),
        V((15, 8, QD), BF16),
        V((2, 4, 4, 4, 8, QD), BF16),
        V((512, 128), BF16),
        V((2, 128, 4 * UNITS), F32),
        V((2, 128, 1), F32),
        V((256, 2 * UNITS), BF16),
        V((4, 2, 4, 4, 8, QD), BF16),
        V((4, 2, 4, 8, QD), BF16),
        V((4, 2, 2, 4, 8, QD), BF16),
        V((4, 2, 4, 8, QD), BF16),
        V((4, 2, 3, 8, QD), BF16),
        V((8, 2, D), BF16),
        V((7, 2, D), BF16),
        V((2, D), F32),
        V((1, D), F32),
        V((128, 4096), BF16),
        V((4096, 256), BF16),
        S((11,)),
        S((15,)), S((15,)), S((8,)), S((8,)), S((15,)), S((15,)),
        S((7,)), S((7,)), S((2, 3)), S((2, 3)), S((2, 4, 3)), S((2, 4, 3)),
        S((3,)), S((3,)), S((4, 2)), S((4, 2)), S((4, 2, 2)), S((4, 2, 2)), S((4, 2, 3)), S((4, 2, 3)), S((7,)), S((7,)),
    ]
    return pl.pallas_call(
        kernel,
        out_shape=jax.ShapeDtypeStruct((2, D), BF16),
        in_specs=[hbm] * 11,
        out_specs=vmem,
        scratch_shapes=scratch,
        compiler_params=pltpu.CompilerParams(
            collective_id=0, has_side_effects=True, vmem_limit_bytes=56 << 20
        ),
        name="layer",
    )(
        hidden_in,
        query,
        kv_map.reshape(4, 128),
        lengths.reshape(4, 128),
        width_class,
        norm_gain.reshape(36, 128),
        kv_pool.reshape(4096, 128),
        o_weight,
        jnp.transpose(gate_weight),
        jnp.transpose(up_weight),
        down_weight,
    )


def solution(mesh):
    placed = (
        P(("seq", "tp"), None),
        P("seq", "tp"),
        P("seq", None, "tp", None, None),
        P(None, "seq"),
        P(),
        P("tp", None),
        P(),
        P(),
        P(None, ("seq", "tp")),
        P(None, ("seq", "tp")),
        P(("seq", "tp"), None),
    )
    return jax.shard_map(
        body, mesh=mesh, in_specs=placed, out_specs=P(("seq", "tp"), None), check_vma=False
    )
```

```python
import functools

import jax
import jax.numpy as jnp
from jax import lax
from jax.experimental import pallas as pl
from jax.experimental.pallas import tpu as pltpu
from jax.sharding import PartitionSpec as P

D = 4608
FF = 36864
WIDTHS = 4
QPRE = 144
SOFTCAP = 50.0
EPS = 1e-06
QD = D // 4
UNITS = FF // 256
MESH = pl.DeviceIdType.MESH
F32 = jnp.float32
BF16 = jnp.bfloat16


def dev(x, y, z, c):
    return (y * 4 + (z // 4) * 2 + c, x * 4 + z % 4)


def dot_nt(a, b):
    return lax.dot_general(a, b, (((1,), (1,)), ((), ())), preferred_element_type=F32)


def remote(src, dst, ssem, rsem, target):
    return pltpu.make_async_remote_copy(
        src_ref=src, dst_ref=dst, send_sem=ssem, recv_sem=rsem, device_id=target, device_id_type=MESH
    )


def kernel(
    hid_hbm, q_hbm, kvm_hbm, len_hbm, wc_hbm, gain_hbm, kv_hbm, ow_hbm, wg_hbm, wu_hbm, wd_hbm,
    out_ref,
    hid_ref, kvm_ref, len_ref, wc_ref, gain_ref, kv_v, ow_v, wgu_v, wd_v,
    qb, oh, oht, qs, ls, ns, nb, nr, nrx, sb, rb, g, xs, acc, ssq, hs, p, rl, rx1, t, rx2, zb, rx3, res, gain, kvt, vs,
    lsem, a1s, a1r, a3s, a3r, bs, br, c1s, c1r, c2s, c2r, c3s, c3r,
    wxs, wxr, d0s, d0r, d1s, d1r, d2s, d2r, d3s, d3r,
):
    seq = lax.axis_index("seq")
    tp = lax.axis_index("tp")
    y, zh, c = seq // 4, (seq // 2) % 2, seq % 2
    x, zl = tp // 4, tp % 4
    z = zh * 4 + zl
    sib = dev(x, y, z, 1 - c)

    seq_offs = [(2, 1), (1, 1), (3, 1), (0, 1), (2, 0), (1, 0), (3, 0)]
    tp_offs = [(dx, dl) for dx in (2, 1, 3, 0) for dl in (2, 1, 3, 0) if (dx, dl) != (0, 0)]
    peers = [sib]
    peers += [dev(x, (y + dy) % 4, ((zh + dh) % 2) * 4 + zl, c) for dy, dh in seq_offs]
    peers += [dev((x + dx) % 4, y, zh * 4 + (zl + dl) % 4, c) for dx, dl in tp_offs]
    peers += [dev(x, y, (1 - zh) * 4 + (zl + dl) % 4, c) for dl in (1, 2, 3)]
    bar = pltpu.get_barrier_semaphore()
    for peer in peers:
        pl.semaphore_signal(bar, inc=1, device_id=peer, device_id_type=MESH)

    loads = [
        pltpu.make_async_copy(kv_hbm, kv_v, lsem.at[0]),
        pltpu.make_async_copy(ow_hbm, ow_v, lsem.at[1]),
        pltpu.make_async_copy(wg_hbm, wgu_v.at[0, c], lsem.at[2]),
        pltpu.make_async_copy(wu_hbm, wgu_v.at[1, c], lsem.at[3]),
        pltpu.make_async_copy(wd_hbm, wd_v.at[c], lsem.at[4]),
    ]
    small = [
        pltpu.make_async_copy(q_hbm, qb.at[seq], lsem.at[5]),
        pltpu.make_async_copy(kvm_hbm, kvm_ref, lsem.at[6]),
        pltpu.make_async_copy(len_hbm, len_ref, lsem.at[7]),
        pltpu.make_async_copy(gain_hbm, gain_ref, lsem.at[8]),
        pltpu.make_async_copy(hid_hbm, hid_ref, lsem.at[9]),
        pltpu.make_async_copy(wc_hbm, wc_ref, lsem.at[10]),
    ]
    for load in small + loads:
        load.start()
    for load in small:
        load.wait()
    pl.semaphore_wait(bar, len(peers))

    sends = []
    a1 = []
    for i, (dy, dh) in enumerate(seq_offs):
        to = dev(x, (y + dy) % 4, ((zh + dh) % 2) * 4 + zl, c)
        cp = remote(qb.at[seq], qb.at[seq], a1s.at[i], a1r.at[i], to)
        cp.start()
        sends.append(cp)
    cp = remote(qb.at[seq], qb.at[seq], a1s.at[7], a1r.at[7], sib)
    cp.start()
    sends.append(cp)

    row_id = lax.broadcasted_iota(jnp.int32, (512, 128), 0).astype(F32)
    lane_id = lax.broadcasted_iota(jnp.int32, (128, 128), 1).astype(F32)
    for j in range(4):
        kvrow = kvm_ref[pl.ds(j, 1), :].astype(F32)
        oh[:, pl.ds(j * 128, 128)] = jnp.where(row_id == kvrow, 1.0, 0.0).astype(BF16)
        kvcol = jnp.transpose(jnp.broadcast_to(kvrow, (128, 128)))
        for k in range(4):
            oht[pl.ds(j * 128, 128), pl.ds(k * 128, 128)] = jnp.where(
                kvcol == lane_id + float(k * 128), 1.0, 0.0
            ).astype(BF16)
        lrow = len_ref[pl.ds(j, 1), :].astype(F32)
        xs[pl.ds(j * 128, 128), pl.ds(0, 128)] = jnp.transpose(
            jnp.broadcast_to(lrow, (128, 128))
        ).astype(BF16)
    for j in range(36):
        gain[:, pl.ds(j * 128, 128)] = gain_ref[pl.ds(j, 1), :]
    ls[...] = jnp.dot(oh[...], xs[:, pl.ds(0, 128)], preferred_element_type=F32)

    loads[0].wait()

    def prepare(blk, _):
        rows = pl.ds(pl.multiple_of(blk * 256, 256), 256)
        block = kv_v[rows, :].astype(F32)
        kvt[:, rows] = jnp.transpose(block).astype(BF16)
        vs[rows, pl.ds(0, 128)] = pltpu.roll(block, 252, 0).astype(BF16)
        vs[rows, pl.ds(128, 128)] = jnp.ones((256, 128), BF16)
        return 0

    lax.fori_loop(0, 16, prepare, 0)
    for i, (dy, dh) in reversed(list(enumerate(seq_offs))):
        frm = ((y - dy) % 4) * 4 + ((zh + dh) % 2) * 2 + c
        a = remote(qb.at[seq], qb.at[frm], a1s.at[i], a1r.at[i], sib)
        a.wait_recv()
        cp = remote(qb.at[frm], qb.at[frm], a1s.at[8 + i], a1r.at[8 + i], sib)
        cp.start()
        sends.append(cp)
    remote(qb.at[seq], qb.at[seq], a1s.at[7], a1r.at[7], sib).wait_recv()
    for i, (dy, dh) in enumerate(seq_offs):
        frm = ((y - dy) % 4) * 4 + ((zh + dh) % 2) * 2 + (1 - c)
        remote(qb.at[frm], qb.at[frm], a1s.at[8 + i], a1r.at[8 + i], sib).wait_recv()

    weights = [
        remote(wg_hbm, wgu_v.at[0, c], wxs.at[0], wxr.at[0], sib),
        remote(wu_hbm, wgu_v.at[1, c], wxs.at[1], wxr.at[1], sib),
        remote(wd_hbm, wd_v.at[c], wxs.at[2], wxr.at[2], sib),
    ]
    sends += weights
    qs[...] = jnp.dot(
        oh[...], qb[...].reshape(512, 256), preferred_element_type=F32
    ).astype(BF16)

    first = seq * 4
    a_id = lax.broadcasted_iota(jnp.int32, (64, 256), 0) & 31
    b_id = lax.broadcasted_iota(jnp.int32, (64, 256), 1)
    own = (a_id == (b_id >> 3)) & ((b_id & 4) == 0)
    pos = (first + (b_id & 3)).astype(F32)
    lane = lax.broadcasted_iota(jnp.int32, (32, 128), 1)

    def attend(blk, _):
        rows = pl.ds(pl.multiple_of(blk * 32, 32), 32)
        span = pl.ds(pl.multiple_of(blk * 256, 256), 256)
        qq = jnp.concatenate([qs[rows, pl.ds(0, 128)], qs[rows, pl.ds(128, 128)]], axis=0)
        s = jnp.dot(qq, kvt[:, span], preferred_element_type=F32)
        e = jnp.exp(SOFTCAP * jnp.tanh(s * (QPRE ** (-0.5) / SOFTCAP)))
        lb = ls[rows, :]
        lb = jnp.concatenate([lb, lb], axis=0)
        lb = jnp.concatenate([lb, lb], axis=1)
        w = jnp.where(own & (pos < lb), e, 0.0)
        low = w.astype(BF16)
        rest = (w - low.astype(F32)).astype(BF16)
        num = jnp.dot(jnp.concatenate([low, rest], axis=0), vs[span, :], preferred_element_type=F32)
        ns[rows, pl.ds(0, 128)] = num[:32, :128].astype(BF16)
        ns[rows, pl.ds(128, 128)] = num[32:64, :128].astype(BF16)
        tot = num[:64, 128:] + num[64:, 128:]
        both = jnp.where((lane & 63) < 32, tot[:32], tot[32:])
        hi = both.astype(BF16).astype(F32)
        ns[rows, pl.ds(256, 128)] = jnp.where(lane < 64, hi, both - hi).astype(BF16)
        return 0

    lax.fori_loop(0, 16, attend, 0, unroll=8)

    for k in range(4):
        v = jnp.dot(
            oht[pl.ds(k * 128, 128), :], ns[...], preferred_element_type=F32
        ).astype(BF16)
        for h in range(2):
            for cc in range(2):
                at = (h * 2 + cc) * 32
                nb[cc, k * 2 + h] = v[at : at + 32]
    cp = remote(nb.at[1 - c], nr, a3s.at[7], a3r.at[7], sib)
    cp.start()
    sends.append(cp)
    cp.wait_recv()

    low_half = lax.broadcasted_iota(jnp.int32, (32, 128), 1) < 64

    def split_total(block):
        both = block + pltpu.roll(block, 64, 1)
        hi = both.astype(BF16).astype(F32)
        return both, jnp.where(low_half, hi, both - hi).astype(BF16)

    def pair_sum(k):
        v = nb[c, k].astype(F32) + nr[k].astype(F32)
        nb[c, k, :, pl.ds(0, 256)] = v[:, :256].astype(BF16)
        nb[c, k, :, pl.ds(256, 128)] = split_total(v[:, 256:])[1]

    a3 = []
    for i, (dy, dh) in enumerate(seq_offs):
        yt, ht = (y + dy) % 4, (zh + dh) % 2
        pair_sum(yt * 2 + ht)
        cp = remote(nb.at[c, yt * 2 + ht], nrx.at[i], a3s.at[i], a3r.at[i], dev(x, yt, ht * 4 + zl, c))
        cp.start()
        sends.append(cp)
        a3.append(cp)
    pair_sum(y * 2 + zh)
    weights[0].start()
    weights[1].start()
    total = nb[c, y * 2 + zh].astype(F32)
    for i in reversed(range(7)):
        a3[i].wait_recv()
        total = total + nrx[i].astype(F32)
    tot = split_total(total[:, 256:])[0]
    att = jnp.concatenate(
        [total[:, :128] / tot[:, 0:1], total[:, 128:256] / tot[:, 32:33]], axis=1
    ).astype(BF16)

    loads[1].wait()
    rid = lax.broadcasted_iota(jnp.int32, (32, QD), 0)
    row0 = x * 8 + zl * 2
    bcp = []
    for dx in (2, 1, 3, 0):
        xt = (x + dx) % 4
        cols = pl.ds(pl.multiple_of(xt * QD, 128), QD)
        v = jnp.dot(att, ow_v[:, cols], preferred_element_type=F32)
        hid = hid_ref[:, cols].astype(F32)
        v = v + jnp.where(rid == row0, hid[0:1], 0.0) + jnp.where(rid == row0 + 1, hid[1:2], 0.0)
        for b in range(4):
            sb[xt, b] = v[b * 8 : b * 8 + 8].astype(BF16)
        for dl in (2, 1, 3, 0):
            if (dx, dl) == (0, 0):
                continue
            i = tp_offs.index((dx, dl))
            lt = (zl + dl) % 4
            cp = remote(sb.at[xt, lt], rb.at[i], bs.at[i], br.at[i], dev(xt, y, zh * 4 + lt, c))
            cp.start()
            sends.append(cp)
            bcp.append(cp)
    weights[2].start()
    v = sb[x, zl].astype(F32)
    for i in range(15):
        bcp[i].wait_recv()
        v = v + rb[i].astype(F32)
    outer, inner = (x, y), (y, x)
    own_piece = g.at[zh, x * (1 - zh) + y * zh, y * (1 - zh) + x * zh, zl]
    own_piece[...] = v.astype(BF16)

    def step(h, along_outer, k):
        if (h == 0) == along_outer:
            return dev((x + k) % 4, y, z, c)
        return dev(x, (y + k) % 4, z, c)

    def push(src, dst, ssem, rsem, to):
        cp = remote(src, dst, ssem, rsem, to)
        cp.start()
        sends.append(cp)

    for k in (4, 3, 5, 2, 6, 1, 7):
        push(own_piece, own_piece, c1s.at[k - 1], c1r.at[k - 1], dev(x, y, (z + k) % 8, c))
    acc[...] = jnp.zeros_like(acc)
    ssq[...] = jnp.zeros_like(ssq)
    for load in loads[2:]:
        load.wait()
    for weight in weights:
        weight.wait_recv()
    for half, blocks in ((zh, [(zl + d) % 4 for d in (1, 3, 2)]), (1 - zh, range(4))):
        ho, hi_ = x * (1 - half) + y * half, y * (1 - half) + x * half
        for m in blocks:
            k = (z + 7 - half * 4 - m) % 8
            piece = g.at[half, ho, hi_, m]
            remote(piece, piece, c1s.at[k], c1r.at[k], sib).wait_recv()
        run = g.at[half, ho, hi_]
        for k in (2, 1, 3):
            to = dev((x + k * half) % 4, (y + k * (1 - half)) % 4, z, c)
            push(run, run, c2s.at[half, k - 1], c2r.at[half, k - 1], to)
        for k in (1, 3):
            to = dev((x + k * (1 - half)) % 4, (y + k * half) % 4, z, c)
            push(run, run, c3s.at[half, 0, k - 1], c3r.at[half, 0, k - 1], to)

    def arrived(h, j, k):
        run = g.at[h, (outer[h] + 4 - k) % 4, (inner[h] + 4 - j) % 4]
        remote(run, run, c3s.at[h, j, k - 1], c3r.at[h, j, k - 1], sib).wait_recv()
        return run

    def relay(j, k):
        for h in range(2):
            run = arrived(h, j, k)
            push(run, run, c3s.at[h, j, 1], c3r.at[h, j, 1], step(h, True, k))

    for j in (1, 3, 2):
        for h in range(2):
            run = g.at[h, outer[h], (inner[h] + 4 - j) % 4]
            remote(run, run, c2s.at[h, j - 1], c2r.at[h, j - 1], sib).wait_recv()
            for k in (1, 3):
                push(run, run, c3s.at[h, j, k - 1], c3r.at[h, j, k - 1], step(h, True, k))
    relay(0, 1)

    def partial(h, f, xq):
        cols = pl.ds(pl.multiple_of(xq * QD, 128), QD)
        u = (f.astype(F32).reshape(128, QD) * gain[:, cols]).astype(BF16)
        acc[h] += dot_nt(u, wgu_v[:, :, :, cols].reshape(4 * UNITS, QD))

    def squares(h, f):
        f = f.astype(F32).reshape(128, QD)
        ssq[h] += jnp.sum(f * f, axis=1, keepdims=True)

    def first_half(xq):
        partial(0, g[0, xq], xq)
        squares(0, g[0, xq])

    relay(3, 3)
    relay(1, 1)
    first_half(x)
    relay(2, 3)
    rest = {1: (3, 2), 3: (0, 1), 2: (0, 3, 1, 2)}
    for k in (1, 3, 2):
        for j in rest[k]:
            arrived(0, j, k)
        first_half((x + 4 - k) % 4)
    for k in (1, 3, 2):
        for j in rest[k]:
            arrived(1, j, k)

    def second_half(xq, _):
        partial(1, g[1, :, xq], xq)
        squares(1, g[1, :, xq])
        return 0

    lax.fori_loop(0, 4, second_half, 0)

    row_y = lax.broadcasted_iota(jnp.int32, (128, 2 * UNITS), 0) >> 5
    row_class = jnp.where(
        row_y == 0, wc_ref[0], jnp.where(row_y == 1, wc_ref[1], jnp.where(row_y == 2, wc_ref[2], wc_ref[3]))
    )
    unit_id = lax.broadcasted_iota(jnp.int32, (128, 2 * UNITS), 1)
    pair_base = ((seq - c) * 16 + tp) * UNITS
    unit = pair_base + unit_id + jnp.where(unit_id >= UNITS, 15 * UNITS, 0)
    active = unit < (row_class + 1) * (FF // WIDTHS)
    for h in range(2):
        scale = lax.rsqrt(ssq[h] * (1.0 / D) + EPS)
        gate = acc[h, :, : 2 * UNITS] * scale
        up = acc[h, :, 2 * UNITS :] * scale
        act = 0.5 * gate * (1.0 + jnp.tanh(0.7978845608028654 * (gate + 0.044715 * gate * gate * gate)))
        hs[pl.ds(h * 128, 128), :] = jnp.where(active, act * up, 0.0).astype(BF16)

    def along(k):
        return jnp.where(k < 2, 0, 1)

    def d0(k, h):
        return remote(
            p.at[k, h, (outer[h] + 2) % 4], rl.at[k, h], d0s.at[k, h], d0r.at[k, h],
            step(h, True, 1 + 2 * along(k)),
        )

    def d1(k, h, way):
        off = 1 + 2 * way
        return remote(
            p.at[k, h, (outer[h] + off) % 4], rx1.at[k, h, way],
            d1s.at[k, h, way], d1r.at[k, h, way], step(h, True, off),
        )

    def d2(k, h, off):
        return remote(
            t.at[k, h, (inner[h] + off) % 4], rx2.at[k, h, off - 1],
            d2s.at[k, h, off - 1], d2r.at[k, h, off - 1], step(h, False, off),
        )

    def produce(i, _):
        k = (i % 2) * 2 + i // 2
        cols = pl.ds(pl.multiple_of(k * QD, 128), QD)
        v = jnp.dot(hs[...], wd_v[:, :, cols].reshape(2 * UNITS, QD), preferred_element_type=F32)
        v = v.astype(BF16).reshape(2, 4, 4, 8, QD)
        for w in range(4):
            p[k, 0, w] = v[0, :, w]
        p[k, 1] = v[1]
        for h in range(2):
            d0(k, h).start()
            d1(k, h, 1 - along(k)).start()
        return 0

    lax.fori_loop(0, 4, produce, 0)

    def combine(i, _):
        k = (i % 2) * 2 + i // 2
        for h in range(2):
            d0(k, h).wait_recv()
            at = (outer[h] + 1 + 2 * along(k)) % 4
            p[k, h, at] = (p[k, h, at].astype(F32) + rl[k, h].astype(F32)).astype(BF16)
            d1(k, h, along(k)).start()
        return 0

    lax.fori_loop(0, 4, combine, 0)

    rid8 = lax.broadcasted_iota(jnp.int32, (8, QD), 0)

    def own_rows(k, _):
        v = g[zh, k * (1 - zh) + y * zh, y * (1 - zh) + k * zh, x].astype(F32)
        cols = pl.ds(pl.multiple_of(k * QD, 128), QD)
        res[pl.ds(0, 1), cols] = jnp.sum(jnp.where(rid8 == zl * 2, v, 0.0), axis=0, keepdims=True)
        res[pl.ds(1, 1), cols] = jnp.sum(jnp.where(rid8 == zl * 2 + 1, v, 0.0), axis=0, keepdims=True)
        return 0

    lax.fori_loop(0, 4, own_rows, 0)

    def outer_sum(i, _):
        k = (i % 2) * 2 + i // 2
        for h in range(2):
            for way in range(2):
                d1(k, h, way).wait_recv()
            v = p[k, h, outer[h]].astype(F32)
            for j in range(2):
                v = v + rx1[k, h, j].astype(F32)
            t[k, h] = v.astype(BF16)
            for off in (2, 1, 3):
                d2(k, h, off).start()
        return 0

    lax.fori_loop(0, 4, outer_sum, 0)

    def inner_sum(k, _):
        cols = pl.ds(pl.multiple_of(k * QD, 128), QD)
        for h in range(2):
            for off in (1, 3, 2):
                d2(k, h, off).wait_recv()
            v = t[k, h, inner[h]].astype(F32)
            for j in range(3):
                v = v + rx2[k, h, j].astype(F32)
            for b in range(4):
                zb[h * 4 + b, :, cols] = v[b * 2 : b * 2 + 2].astype(BF16)
        return 0

    lax.fori_loop(0, 4, inner_sum, 0)
    d3 = []
    for k in (4, 3, 5, 2, 6, 1, 7):
        zt = (z + k) % 8
        cp = remote(zb.at[zt], rx3.at[k - 1], d3s.at[k - 1], d3r.at[k - 1], dev(x, y, zt, c))
        cp.start()
        sends.append(cp)
        d3.append(cp)
    v = zb[z].astype(F32) + res[...]
    for cp in d3:
        cp.wait_recv()
    for k in range(7):
        v = v + rx3[k].astype(F32)
    out_ref[...] = v.astype(BF16)
    for cp in sends:
        cp.wait_send()

    def drain(k, _):
        for h in range(2):
            d0(k, h).wait_send()
            for way in range(2):
                d1(k, h, way).wait_send()
            for off in (1, 2, 3):
                d2(k, h, off).wait_send()
        return 0

    lax.fori_loop(0, 4, drain, 0)


def body(
    hidden_in, query, kv_pool, kv_map, lengths, o_weight, norm_gain, width_class,
    gate_weight, up_weight, down_weight,
):
    vmem = pl.BlockSpec(memory_space=pltpu.VMEM)
    hbm = pl.BlockSpec(memory_space=pl.ANY)
    V, S = pltpu.VMEM, pltpu.SemaphoreType.DMA
    scratch = [
        V((2, D), BF16), V((4, 128), jnp.int32), V((4, 128), jnp.int32), pltpu.SMEM((4,), jnp.int32),
        V((36, 128), F32),
        V((4096, 128), BF16), V((256, D), BF16), V((2, 2, UNITS, D), BF16), V((2, UNITS, D), BF16),
        V((16, 32, 256), BF16),
        V((512, 512), BF16),
        V((512, 512), BF16),
        V((512, 256), BF16),
        V((512, 128), F32),
        V((512, 384), BF16),
        V((2, 8, 32, 384), BF16),
        V((8, 32, 384), BF16),
        V((7, 32, 384), BF16),
        V((4, 4, 8, QD), BF16),
        V((15, 8, QD), BF16),
        V((2, 4, 4, 4, 8, QD), BF16),
        V((512, 128), BF16),
        V((2, 128, 4 * UNITS), F32),
        V((2, 128, 1), F32),
        V((256, 2 * UNITS), BF16),
        V((4, 2, 4, 4, 8, QD), BF16),
        V((4, 2, 4, 8, QD), BF16),
        V((4, 2, 2, 4, 8, QD), BF16),
        V((4, 2, 4, 8, QD), BF16),
        V((4, 2, 3, 8, QD), BF16),
        V((8, 2, D), BF16),
        V((7, 2, D), BF16),
        V((2, D), F32),
        V((1, D), F32),
        V((128, 4096), BF16),
        V((4096, 256), BF16),
        S((11,)),
        S((15,)), S((15,)), S((8,)), S((8,)), S((15,)), S((15,)),
        S((7,)), S((7,)), S((2, 3)), S((2, 3)), S((2, 4, 3)), S((2, 4, 3)),
        S((3,)), S((3,)), S((4, 2)), S((4, 2)), S((4, 2, 2)), S((4, 2, 2)), S((4, 2, 3)), S((4, 2, 3)), S((7,)), S((7,)),
    ]
    return pl.pallas_call(
        kernel,
        out_shape=jax.ShapeDtypeStruct((2, D), BF16),
        in_specs=[hbm] * 11,
        out_specs=vmem,
        scratch_shapes=scratch,
        compiler_params=pltpu.CompilerParams(
            collective_id=0, has_side_effects=True, vmem_limit_bytes=56 << 20
        ),
        name="layer",
    )(
        hidden_in,
        query,
        kv_map.reshape(4, 128),
        lengths.reshape(4, 128),
        width_class,
        norm_gain.reshape(36, 128),
        kv_pool.reshape(4096, 128),
        o_weight,
        jnp.transpose(gate_weight),
        jnp.transpose(up_weight),
        down_weight,
    )


def solution(mesh):
    placed = (
        P(("seq", "tp"), None),
        P("seq", "tp"),
        P("seq", None, "tp", None, None),
        P(None, "seq"),
        P(),
        P("tp", None),
        P(),
        P(),
        P(None, ("seq", "tp")),
        P(None, ("seq", "tp")),
        P(("seq", "tp"), None),
    )
    return jax.shard_map(
        body, mesh=mesh, in_specs=placed, out_specs=P(("seq", "tp"), None), check_vma=False
    )
```

```python
import functools

import jax
import jax.numpy as jnp
from jax import lax
from jax.experimental import pallas as pl
from jax.experimental.pallas import tpu as pltpu
from jax.sharding import PartitionSpec as P

D = 4608
FF = 36864
WIDTHS = 4
QPRE = 144
SOFTCAP = 50.0
EPS = 1e-06
QD = D // 4
UNITS = FF // 256
MESH = pl.DeviceIdType.MESH
F32 = jnp.float32
BF16 = jnp.bfloat16


def dev(x, y, z, c):
    return (y * 4 + (z // 4) * 2 + c, x * 4 + z % 4)


def dot_nt(a, b):
    return lax.dot_general(a, b, (((1,), (1,)), ((), ())), preferred_element_type=F32)


def remote(src, dst, ssem, rsem, target):
    return pltpu.make_async_remote_copy(
        src_ref=src, dst_ref=dst, send_sem=ssem, recv_sem=rsem, device_id=target, device_id_type=MESH
    )


def kernel(
    hid_hbm, q_hbm, kvm_hbm, len_hbm, wc_hbm, gain_hbm, kv_hbm, ow_hbm, wg_hbm, wu_hbm, wd_hbm,
    out_ref,
    hid_ref, kvm_ref, len_ref, wc_ref, gain_ref, kv_v, ow_v, wgu_v, wd_v,
    qb, oh, oht, qs, ls, ns, nb, nr, nrx, sb, rb, g, xs, acc, ssq, hs, p, rl, rx1, t, rx2, zb, rx3, res, gain, kvt, vs,
    lsem, a1s, a1r, a3s, a3r, bs, br, c1s, c1r, c2s, c2r, c3s, c3r,
    wxs, wxr, d0s, d0r, d1s, d1r, d2s, d2r, d3s, d3r,
):
    seq = lax.axis_index("seq")
    tp = lax.axis_index("tp")
    y, zh, c = seq // 4, (seq // 2) % 2, seq % 2
    x, zl = tp // 4, tp % 4
    z = zh * 4 + zl
    sib = dev(x, y, z, 1 - c)

    seq_offs = [(2, 1), (1, 1), (3, 1), (0, 1), (2, 0), (1, 0), (3, 0)]
    tp_offs = [(dx, dl) for dx in (2, 1, 3, 0) for dl in (2, 1, 3, 0) if (dx, dl) != (0, 0)]
    peers = [sib]
    peers += [dev(x, (y + dy) % 4, ((zh + dh) % 2) * 4 + zl, c) for dy, dh in seq_offs]
    peers += [dev((x + dx) % 4, y, zh * 4 + (zl + dl) % 4, c) for dx, dl in tp_offs]
    peers += [dev(x, y, (1 - zh) * 4 + (zl + dl) % 4, c) for dl in (1, 2, 3)]
    bar = pltpu.get_barrier_semaphore()
    for peer in peers:
        pl.semaphore_signal(bar, inc=1, device_id=peer, device_id_type=MESH)

    loads = [
        pltpu.make_async_copy(kv_hbm, kv_v, lsem.at[0]),
        pltpu.make_async_copy(ow_hbm, ow_v, lsem.at[1]),
        pltpu.make_async_copy(wg_hbm, wgu_v.at[0, c], lsem.at[2]),
        pltpu.make_async_copy(wu_hbm, wgu_v.at[1, c], lsem.at[3]),
        pltpu.make_async_copy(wd_hbm, wd_v.at[c], lsem.at[4]),
    ]
    small = [
        pltpu.make_async_copy(q_hbm, qb.at[seq], lsem.at[5]),
        pltpu.make_async_copy(kvm_hbm, kvm_ref, lsem.at[6]),
        pltpu.make_async_copy(len_hbm, len_ref, lsem.at[7]),
        pltpu.make_async_copy(gain_hbm, gain_ref, lsem.at[8]),
        pltpu.make_async_copy(hid_hbm, hid_ref, lsem.at[9]),
        pltpu.make_async_copy(wc_hbm, wc_ref, lsem.at[10]),
    ]
    for load in small + loads:
        load.start()
    for load in small:
        load.wait()
    pl.semaphore_wait(bar, len(peers))

    sends = []
    a1 = []
    for i, (dy, dh) in enumerate(seq_offs):
        to = dev(x, (y + dy) % 4, ((zh + dh) % 2) * 4 + zl, c)
        cp = remote(qb.at[seq], qb.at[seq], a1s.at[i], a1r.at[i], to)
        cp.start()
        sends.append(cp)
    cp = remote(qb.at[seq], qb.at[seq], a1s.at[7], a1r.at[7], sib)
    cp.start()
    sends.append(cp)

    row_id = lax.broadcasted_iota(jnp.int32, (512, 128), 0).astype(F32)
    lane_id = lax.broadcasted_iota(jnp.int32, (128, 128), 1).astype(F32)
    for j in range(4):
        kvrow = kvm_ref[pl.ds(j, 1), :].astype(F32)
        oh[:, pl.ds(j * 128, 128)] = jnp.where(row_id == kvrow, 1.0, 0.0).astype(BF16)
        kvcol = jnp.transpose(jnp.broadcast_to(kvrow, (128, 128)))
        for k in range(4):
            oht[pl.ds(j * 128, 128), pl.ds(k * 128, 128)] = jnp.where(
                kvcol == lane_id + float(k * 128), 1.0, 0.0
            ).astype(BF16)
        lrow = len_ref[pl.ds(j, 1), :].astype(F32)
        xs[pl.ds(j * 128, 128), pl.ds(0, 128)] = jnp.transpose(
            jnp.broadcast_to(lrow, (128, 128))
        ).astype(BF16)
    for j in range(36):
        gain[:, pl.ds(j * 128, 128)] = gain_ref[pl.ds(j, 1), :]
    ls[...] = jnp.dot(oh[...], xs[:, pl.ds(0, 128)], preferred_element_type=F32)

    loads[0].wait()

    def prepare(blk, _):
        rows = pl.ds(pl.multiple_of(blk * 256, 256), 256)
        block = kv_v[rows, :].astype(F32)
        kvt[:, rows] = jnp.transpose(block).astype(BF16)
        vs[rows, pl.ds(0, 128)] = pltpu.roll(block, 252, 0).astype(BF16)
        vs[rows, pl.ds(128, 128)] = jnp.ones((256, 128), BF16)
        return 0

    lax.fori_loop(0, 16, prepare, 0)
    for i, (dy, dh) in reversed(list(enumerate(seq_offs))):
        frm = ((y - dy) % 4) * 4 + ((zh + dh) % 2) * 2 + c
        a = remote(qb.at[seq], qb.at[frm], a1s.at[i], a1r.at[i], sib)
        a.wait_recv()
        cp = remote(qb.at[frm], qb.at[frm], a1s.at[8 + i], a1r.at[8 + i], sib)
        cp.start()
        sends.append(cp)
    remote(qb.at[seq], qb.at[seq], a1s.at[7], a1r.at[7], sib).wait_recv()
    for i, (dy, dh) in enumerate(seq_offs):
        frm = ((y - dy) % 4) * 4 + ((zh + dh) % 2) * 2 + (1 - c)
        remote(qb.at[frm], qb.at[frm], a1s.at[8 + i], a1r.at[8 + i], sib).wait_recv()

    weights = [
        remote(wg_hbm, wgu_v.at[0, c], wxs.at[0], wxr.at[0], sib),
        remote(wu_hbm, wgu_v.at[1, c], wxs.at[1], wxr.at[1], sib),
        remote(wd_hbm, wd_v.at[c], wxs.at[2], wxr.at[2], sib),
    ]
    sends += weights
    qs[...] = jnp.dot(
        oh[...], qb[...].reshape(512, 256), preferred_element_type=F32
    ).astype(BF16)

    first = seq * 4
    a_id = lax.broadcasted_iota(jnp.int32, (64, 256), 0) & 31
    b_id = lax.broadcasted_iota(jnp.int32, (64, 256), 1)
    own = (a_id == (b_id >> 3)) & ((b_id & 4) == 0)
    pos = (first + (b_id & 3)).astype(F32)
    lane = lax.broadcasted_iota(jnp.int32, (32, 128), 1)

    def attend(blk, _):
        rows = pl.ds(pl.multiple_of(blk * 32, 32), 32)
        span = pl.ds(pl.multiple_of(blk * 256, 256), 256)
        qq = jnp.concatenate([qs[rows, pl.ds(0, 128)], qs[rows, pl.ds(128, 128)]], axis=0)
        s = jnp.dot(qq, kvt[:, span], preferred_element_type=F32)
        e = jnp.exp(SOFTCAP * jnp.tanh(s * (QPRE ** (-0.5) / SOFTCAP)))
        lb = ls[rows, :]
        lb = jnp.concatenate([lb, lb], axis=0)
        lb = jnp.concatenate([lb, lb], axis=1)
        w = jnp.where(own & (pos < lb), e, 0.0)
        low = w.astype(BF16)
        rest = (w - low.astype(F32)).astype(BF16)
        num = jnp.dot(jnp.concatenate([low, rest], axis=0), vs[span, :], preferred_element_type=F32)
        ns[rows, pl.ds(0, 128)] = num[:32, :128].astype(BF16)
        ns[rows, pl.ds(128, 128)] = num[32:64, :128].astype(BF16)
        tot = num[:64, 128:] + num[64:, 128:]
        both = jnp.where((lane & 63) < 32, tot[:32], tot[32:])
        hi = both.astype(BF16).astype(F32)
        ns[rows, pl.ds(256, 128)] = jnp.where(lane < 64, hi, both - hi).astype(BF16)
        return 0

    lax.fori_loop(0, 16, attend, 0, unroll=8)

    for k in range(4):
        v = jnp.dot(
            oht[pl.ds(k * 128, 128), :], ns[...], preferred_element_type=F32
        ).astype(BF16)
        for h in range(2):
            for cc in range(2):
                at = (h * 2 + cc) * 32
                nb[cc, k * 2 + h] = v[at : at + 32]
    cp = remote(nb.at[1 - c], nr, a3s.at[7], a3r.at[7], sib)
    cp.start()
    sends.append(cp)
    cp.wait_recv()

    low_half = lax.broadcasted_iota(jnp.int32, (32, 128), 1) < 64

    def split_total(block):
        both = block + pltpu.roll(block, 64, 1)
        hi = both.astype(BF16).astype(F32)
        return both, jnp.where(low_half, hi, both - hi).astype(BF16)

    def pair_sum(k):
        v = nb[c, k].astype(F32) + nr[k].astype(F32)
        nb[c, k, :, pl.ds(0, 256)] = v[:, :256].astype(BF16)
        nb[c, k, :, pl.ds(256, 128)] = split_total(v[:, 256:])[1]

    a3 = []
    for i, (dy, dh) in enumerate(seq_offs):
        yt, ht = (y + dy) % 4, (zh + dh) % 2
        pair_sum(yt * 2 + ht)
        cp = remote(nb.at[c, yt * 2 + ht], nrx.at[i], a3s.at[i], a3r.at[i], dev(x, yt, ht * 4 + zl, c))
        cp.start()
        sends.append(cp)
        a3.append(cp)
    pair_sum(y * 2 + zh)
    weights[0].start()
    weights[1].start()
    total = nb[c, y * 2 + zh].astype(F32)
    for i in reversed(range(7)):
        a3[i].wait_recv()
        total = total + nrx[i].astype(F32)
    tot = split_total(total[:, 256:])[0]
    att = jnp.concatenate(
        [total[:, :128] / tot[:, 0:1], total[:, 128:256] / tot[:, 32:33]], axis=1
    ).astype(BF16)

    loads[1].wait()
    rid = lax.broadcasted_iota(jnp.int32, (32, QD), 0)
    row0 = x * 8 + zl * 2
    bcp = []
    for dx in (2, 1, 3, 0):
        xt = (x + dx) % 4
        cols = pl.ds(pl.multiple_of(xt * QD, 128), QD)
        v = jnp.dot(att, ow_v[:, cols], preferred_element_type=F32)
        hid = hid_ref[:, cols].astype(F32)
        v = v + jnp.where(rid == row0, hid[0:1], 0.0) + jnp.where(rid == row0 + 1, hid[1:2], 0.0)
        for b in range(4):
            sb[xt, b] = v[b * 8 : b * 8 + 8].astype(BF16)
        for dl in (2, 1, 3, 0):
            if (dx, dl) == (0, 0):
                continue
            i = tp_offs.index((dx, dl))
            lt = (zl + dl) % 4
            cp = remote(sb.at[xt, lt], rb.at[i], bs.at[i], br.at[i], dev(xt, y, zh * 4 + lt, c))
            cp.start()
            sends.append(cp)
            bcp.append(cp)
    weights[2].start()
    v = sb[x, zl].astype(F32)
    for i in range(15):
        bcp[i].wait_recv()
        v = v + rb[i].astype(F32)
    outer, inner = (x, y), (y, x)
    own_piece = g.at[zh, x * (1 - zh) + y * zh, y * (1 - zh) + x * zh, zl]
    own_piece[...] = v.astype(BF16)

    def step(h, along_outer, k):
        if (h == 0) == along_outer:
            return dev((x + k) % 4, y, z, c)
        return dev(x, (y + k) % 4, z, c)

    def push(src, dst, ssem, rsem, to):
        cp = remote(src, dst, ssem, rsem, to)
        cp.start()
        sends.append(cp)

    for k in (4, 3, 5, 2, 6, 1, 7):
        push(own_piece, own_piece, c1s.at[k - 1], c1r.at[k - 1], dev(x, y, (z + k) % 8, c))
    acc[...] = jnp.zeros_like(acc)
    ssq[...] = jnp.zeros_like(ssq)
    for load in loads[2:]:
        load.wait()
    for weight in weights:
        weight.wait_recv()
    for half, blocks in ((zh, [(zl + d) % 4 for d in (1, 3, 2)]), (1 - zh, range(4))):
        ho, hi_ = x * (1 - half) + y * half, y * (1 - half) + x * half
        for m in blocks:
            k = (z + 7 - half * 4 - m) % 8
            piece = g.at[half, ho, hi_, m]
            remote(piece, piece, c1s.at[k], c1r.at[k], sib).wait_recv()
        run = g.at[half, ho, hi_]
        for k in (2, 1, 3):
            to = dev((x + k * half) % 4, (y + k * (1 - half)) % 4, z, c)
            push(run, run, c2s.at[half, k - 1], c2r.at[half, k - 1], to)
        for k in (1, 3):
            to = dev((x + k * (1 - half)) % 4, (y + k * half) % 4, z, c)
            push(run, run, c3s.at[half, 0, k - 1], c3r.at[half, 0, k - 1], to)

    def arrived(h, j, k):
        run = g.at[h, (outer[h] + 4 - k) % 4, (inner[h] + 4 - j) % 4]
        remote(run, run, c3s.at[h, j, k - 1], c3r.at[h, j, k - 1], sib).wait_recv()
        return run

    def relay(j, k):
        for h in range(2):
            run = arrived(h, j, k)
            push(run, run, c3s.at[h, j, 1], c3r.at[h, j, 1], step(h, True, k))

    for j in (1, 3, 2):
        for h in range(2):
            run = g.at[h, outer[h], (inner[h] + 4 - j) % 4]
            remote(run, run, c2s.at[h, j - 1], c2r.at[h, j - 1], sib).wait_recv()
            for k in (1, 3):
                push(run, run, c3s.at[h, j, k - 1], c3r.at[h, j, k - 1], step(h, True, k))
    relay(0, 1)

    def partial(h, f, xq):
        cols = pl.ds(pl.multiple_of(xq * QD, 128), QD)
        u = (f.astype(F32).reshape(128, QD) * gain[:, cols]).astype(BF16)
        acc[h] += dot_nt(u, wgu_v[:, :, :, cols].reshape(4 * UNITS, QD))

    def squares(h, f):
        f = f.astype(F32).reshape(128, QD)
        ssq[h] += jnp.sum(f * f, axis=1, keepdims=True)

    def first_half(xq):
        partial(0, g[0, xq], xq)
        squares(0, g[0, xq])

    relay(3, 3)
    relay(1, 1)
    first_half(x)
    relay(2, 3)
    rest = {1: (3, 2), 3: (0, 1), 2: (0, 3, 1, 2)}
    for k in (1, 3, 2):
        for j in rest[k]:
            arrived(0, j, k)
        first_half((x + 4 - k) % 4)
    for k in (1, 3, 2):
        for j in rest[k]:
            arrived(1, j, k)

    def second_half(xq, _):
        partial(1, g[1, :, xq], xq)
        squares(1, g[1, :, xq])
        return 0

    lax.fori_loop(0, 4, second_half, 0)

    row_y = lax.broadcasted_iota(jnp.int32, (128, 2 * UNITS), 0) >> 5
    row_class = jnp.where(
        row_y == 0, wc_ref[0], jnp.where(row_y == 1, wc_ref[1], jnp.where(row_y == 2, wc_ref[2], wc_ref[3]))
    )
    unit_id = lax.broadcasted_iota(jnp.int32, (128, 2 * UNITS), 1)
    pair_base = ((seq - c) * 16 + tp) * UNITS
    unit = pair_base + unit_id + jnp.where(unit_id >= UNITS, 15 * UNITS, 0)
    active = unit < (row_class + 1) * (FF // WIDTHS)
    for h in range(2):
        scale = lax.rsqrt(ssq[h] * (1.0 / D) + EPS)
        gate = acc[h, :, : 2 * UNITS] * scale
        up = acc[h, :, 2 * UNITS :] * scale
        act = 0.5 * gate * (1.0 + jnp.tanh(0.7978845608028654 * (gate + 0.044715 * gate * gate * gate)))
        hs[pl.ds(h * 128, 128), :] = jnp.where(active, act * up, 0.0).astype(BF16)

    def along(k):
        return jnp.where(k < 2, 0, 1)

    def d0(k, h):
        return remote(
            p.at[k, h, (outer[h] + 2) % 4], rl.at[k, h], d0s.at[k, h], d0r.at[k, h],
            step(h, True, 1 + 2 * along(k)),
        )

    def d1(k, h, way):
        off = 1 + 2 * way
        return remote(
            p.at[k, h, (outer[h] + off) % 4], rx1.at[k, h, way],
            d1s.at[k, h, way], d1r.at[k, h, way], step(h, True, off),
        )

    def d2(k, h, off):
        return remote(
            t.at[k, h, (inner[h] + off) % 4], rx2.at[k, h, off - 1],
            d2s.at[k, h, off - 1], d2r.at[k, h, off - 1], step(h, False, off),
        )

    def produce(i, _):
        k = (i % 2) * 2 + i // 2
        cols = pl.ds(pl.multiple_of(k * QD, 128), QD)
        v = jnp.dot(hs[...], wd_v[:, :, cols].reshape(2 * UNITS, QD), preferred_element_type=F32)
        v = v.astype(BF16).reshape(2, 4, 4, 8, QD)
        for w in range(4):
            p[k, 0, w] = v[0, :, w]
        p[k, 1] = v[1]
        for h in range(2):
            d0(k, h).start()
        return 0

    lax.fori_loop(0, 4, produce, 0)

    def direct(i, _):
        k = (i % 2) * 2 + i // 2
        for h in range(2):
            d1(k, h, 1 - along(k)).start()
        return 0

    lax.fori_loop(0, 4, direct, 0)

    def combine(i, _):
        k = (i % 2) * 2 + i // 2
        for h in range(2):
            d0(k, h).wait_recv()
            at = (outer[h] + 1 + 2 * along(k)) % 4
            p[k, h, at] = (p[k, h, at].astype(F32) + rl[k, h].astype(F32)).astype(BF16)
            d1(k, h, along(k)).start()
        return 0

    lax.fori_loop(0, 4, combine, 0)

    rid8 = lax.broadcasted_iota(jnp.int32, (8, QD), 0)

    def own_rows(k, _):
        v = g[zh, k * (1 - zh) + y * zh, y * (1 - zh) + k * zh, x].astype(F32)
        cols = pl.ds(pl.multiple_of(k * QD, 128), QD)
        res[pl.ds(0, 1), cols] = jnp.sum(jnp.where(rid8 == zl * 2, v, 0.0), axis=0, keepdims=True)
        res[pl.ds(1, 1), cols] = jnp.sum(jnp.where(rid8 == zl * 2 + 1, v, 0.0), axis=0, keepdims=True)
        return 0

    lax.fori_loop(0, 4, own_rows, 0)

    def outer_sum(i, _):
        k = (i % 2) * 2 + i // 2
        for h in range(2):
            for way in range(2):
                d1(k, h, way).wait_recv()
            v = p[k, h, outer[h]].astype(F32)
            for j in range(2):
                v = v + rx1[k, h, j].astype(F32)
            t[k, h] = v.astype(BF16)
            for off in (2, 1, 3):
                d2(k, h, off).start()
        return 0

    lax.fori_loop(0, 4, outer_sum, 0)

    def inner_sum(k, _):
        cols = pl.ds(pl.multiple_of(k * QD, 128), QD)
        for h in range(2):
            for off in (1, 3, 2):
                d2(k, h, off).wait_recv()
            v = t[k, h, inner[h]].astype(F32)
            for j in range(3):
                v = v + rx2[k, h, j].astype(F32)
            for b in range(4):
                zb[h * 4 + b, :, cols] = v[b * 2 : b * 2 + 2].astype(BF16)
        return 0

    lax.fori_loop(0, 4, inner_sum, 0)
    d3 = []
    for k in (4, 3, 5, 2, 6, 1, 7):
        zt = (z + k) % 8
        cp = remote(zb.at[zt], rx3.at[k - 1], d3s.at[k - 1], d3r.at[k - 1], dev(x, y, zt, c))
        cp.start()
        sends.append(cp)
        d3.append(cp)
    v = zb[z].astype(F32) + res[...]
    for cp in d3:
        cp.wait_recv()
    for k in range(7):
        v = v + rx3[k].astype(F32)
    out_ref[...] = v.astype(BF16)
    for cp in sends:
        cp.wait_send()

    def drain(k, _):
        for h in range(2):
            d0(k, h).wait_send()
            for way in range(2):
                d1(k, h, way).wait_send()
            for off in (1, 2, 3):
                d2(k, h, off).wait_send()
        return 0

    lax.fori_loop(0, 4, drain, 0)


def body(
    hidden_in, query, kv_pool, kv_map, lengths, o_weight, norm_gain, width_class,
    gate_weight, up_weight, down_weight,
):
    vmem = pl.BlockSpec(memory_space=pltpu.VMEM)
    hbm = pl.BlockSpec(memory_space=pl.ANY)
    V, S = pltpu.VMEM, pltpu.SemaphoreType.DMA
    scratch = [
        V((2, D), BF16), V((4, 128), jnp.int32), V((4, 128), jnp.int32), pltpu.SMEM((4,), jnp.int32),
        V((36, 128), F32),
        V((4096, 128), BF16), V((256, D), BF16), V((2, 2, UNITS, D), BF16), V((2, UNITS, D), BF16),
        V((16, 32, 256), BF16),
        V((512, 512), BF16),
        V((512, 512), BF16),
        V((512, 256), BF16),
        V((512, 128), F32),
        V((512, 384), BF16),
        V((2, 8, 32, 384), BF16),
        V((8, 32, 384), BF16),
        V((7, 32, 384), BF16),
        V((4, 4, 8, QD), BF16),
        V((15, 8, QD), BF16),
        V((2, 4, 4, 4, 8, QD), BF16),
        V((512, 128), BF16),
        V((2, 128, 4 * UNITS), F32),
        V((2, 128, 1), F32),
        V((256, 2 * UNITS), BF16),
        V((4, 2, 4, 4, 8, QD), BF16),
        V((4, 2, 4, 8, QD), BF16),
        V((4, 2, 2, 4, 8, QD), BF16),
        V((4, 2, 4, 8, QD), BF16),
        V((4, 2, 3, 8, QD), BF16),
        V((8, 2, D), BF16),
        V((7, 2, D), BF16),
        V((2, D), F32),
        V((1, D), F32),
        V((128, 4096), BF16),
        V((4096, 256), BF16),
        S((11,)),
        S((15,)), S((15,)), S((8,)), S((8,)), S((15,)), S((15,)),
        S((7,)), S((7,)), S((2, 3)), S((2, 3)), S((2, 4, 3)), S((2, 4, 3)),
        S((3,)), S((3,)), S((4, 2)), S((4, 2)), S((4, 2, 2)), S((4, 2, 2)), S((4, 2, 3)), S((4, 2, 3)), S((7,)), S((7,)),
    ]
    return pl.pallas_call(
        kernel,
        out_shape=jax.ShapeDtypeStruct((2, D), BF16),
        in_specs=[hbm] * 11,
        out_specs=vmem,
        scratch_shapes=scratch,
        compiler_params=pltpu.CompilerParams(
            collective_id=0, has_side_effects=True, vmem_limit_bytes=56 << 20
        ),
        name="layer",
    )(
        hidden_in,
        query,
        kv_map.reshape(4, 128),
        lengths.reshape(4, 128),
        width_class,
        norm_gain.reshape(36, 128),
        kv_pool.reshape(4096, 128),
        o_weight,
        jnp.transpose(gate_weight),
        jnp.transpose(up_weight),
        down_weight,
    )


def solution(mesh):
    placed = (
        P(("seq", "tp"), None),
        P("seq", "tp"),
        P("seq", None, "tp", None, None),
        P(None, "seq"),
        P(),
        P("tp", None),
        P(),
        P(),
        P(None, ("seq", "tp")),
        P(None, ("seq", "tp")),
        P(("seq", "tp"), None),
    )
    return jax.shard_map(
        body, mesh=mesh, in_specs=placed, out_specs=P(("seq", "tp"), None), check_vma=False
    )
```
